256 devices in a mesh: seq: 64 (over y_lo, z, x), chan: 4 (over y_hi, core).
Axes of the slice: x: 4, y: 4 (y_hi: 2, y_lo: 2; y = y_hi * 2 + y_lo), z: 8, core: 2. Of those that a mesh axis runs over, the one named last changes fastest.
Arguments:
- out_gate: bfloat16 [32768, 2048], P('seq', 'chan'), may hold values from -6 to 6
- in_gate: bfloat16 [32768, 2048], P('seq', 'chan'), may hold values from -6 to 6
- values: bfloat16 [32768, 2048], P('seq', 'chan'), may hold values from -6 to 6
- filter_param: bfloat16 [32768, 2048], P('seq', 'chan'), may hold values from -193.49419 to 193.49419
- out_weight: bfloat16 [2048, 2048], P('chan'), may hold values from -0.125 to 0.125
- out_cotangent: bfloat16 [32768, 2048], P(('seq', 'chan')), may hold values from -6 to 6
Outputs:
- output: bfloat16 [32768, 2048], P(('seq', 'chan'))
- d_out_gate: float32 [32768, 2048], P('seq', 'chan')
- d_in_gate: float32 [32768, 2048], P('seq', 'chan')
- d_values: float32 [32768, 2048], P('seq', 'chan')
- d_filter: float32 [32768, 2048], P('seq', 'chan')
The draws below stay inside these ranges and needn't reach their ends.
All inputs are finite; a program needn't handle non-finite values.
Results may differ from the reference program's by a relative error of at most 0.006.
Values may be sent and summed in bfloat16 or wider, within the bound.
A program may use at most 128 MiB of HBM per device.

```python
import math
import jax
import jax.numpy as jnp
from jax import lax

CHANNELS = 2048
DOUT = 2048
SEQUENCE_TOKENS = 32768


def channel_means(key, lowest, highest):
    sign_key, size_key = jax.random.split(key)
    signs = jnp.where(jax.random.bernoulli(sign_key, 0.5, (CHANNELS,)), 1.0, -1.0)
    return signs * jax.random.uniform(size_key, (CHANNELS,), jnp.float32, lowest, highest)


def draw_in_gate(key, part):
    key = jax.random.fold_in(key, 11)
    mean_key, noise_key = jax.random.split(key)
    noise_field = jnp.clip(jax.random.normal(noise_key, (SEQUENCE_TOKENS, CHANNELS), jnp.float32), -4.0, 4.0)
    return jnp.clip(channel_means(mean_key, 1.0, 2.0)[None, :] + noise_field, -6.0, 6.0).astype(jnp.bfloat16)


def draw_values(key, part):
    key = jax.random.fold_in(key, 13)
    mean_key, noise_key = jax.random.split(key)
    noise_field = jnp.clip(jax.random.normal(noise_key, (SEQUENCE_TOKENS, CHANNELS), jnp.float32), -4.0, 4.0)
    return jnp.clip(channel_means(mean_key, 1.0, 2.0)[None, :] + noise_field, -6.0, 6.0).astype(jnp.bfloat16)


def draw_filter_param(key, part):
    key = jax.random.fold_in(key, 7)
    random_subkeys = jax.random.split(key, 8)
    noise_field = jnp.clip(jax.random.normal(random_subkeys[0], (SEQUENCE_TOKENS, CHANNELS), jnp.float32), -4.0, 4.0)
    fast_share = 0.5
    fast_mask = jax.random.bernoulli(random_subkeys[1], fast_share, (CHANNELS,))
    slow_rate = jnp.exp(jax.random.uniform(random_subkeys[2], (CHANNELS,), jnp.float32, math.log(0.3), math.log(2.0))) / SEQUENCE_TOKENS
    fast_rate = jnp.exp(jax.random.uniform(random_subkeys[3], (CHANNELS,), jnp.float32, math.log(1.0 / 50.0), math.log(1.0 / 30.0)))
    decay_rate = jnp.where(fast_mask, fast_rate, slow_rate)
    energy = jnp.expm1(-2.0 * decay_rate * SEQUENCE_TOKENS) / jnp.expm1(-2.0 * decay_rate)
    spike_positions = jax.random.randint(random_subkeys[4], (4,), 0, SEQUENCE_TOKENS)
    dropout_scale = jax.random.uniform(random_subkeys[5], (4, CHANNELS), jnp.float32, 0.5, 0.8)
    floor_share = jnp.exp(jax.random.uniform(random_subkeys[6], (CHANNELS,), jnp.float32, math.log(1e-05), math.log(0.0002)))
    floor_sign = jnp.where(jax.random.bernoulli(random_subkeys[7], 0.5, (CHANNELS,)), 1.0, -1.0)
    floor_level = jnp.where(fast_mask, floor_sign * jnp.sqrt(floor_share), 0.0)
    position_numbers = jnp.arange(SEQUENCE_TOKENS, dtype=jnp.int32)[:, None]
    filter_envelope = jnp.exp(-position_numbers.astype(jnp.float32) * decay_rate)
    for spike_number in range(4):
        filter_envelope = filter_envelope * jnp.where(position_numbers >= spike_positions[spike_number], dropout_scale[spike_number], 1.0)
    return (noise_field * filter_envelope * jnp.sqrt(SEQUENCE_TOKENS / energy) + floor_level[None, :]).astype(jnp.bfloat16)


def levels(key, shape, shards, low, top_value):
    gain = 1.0
    for dim, parts in shards:
        draws = jax.random.uniform(jax.random.fold_in(jax.random.fold_in(key, 6), dim), (parts,), jnp.float32, low / len(shards), top_value / len(shards))
        gain = gain * jnp.repeat(jnp.exp(draws), shape[dim] // parts).reshape((-1,) + (1,) * (len(shape) - 1 - dim))
    return gain


def bell_draw(key, dims, scale, limit, cuts=(), kind=jnp.bfloat16):
    level = levels(key, dims, cuts, -0.22, 0.18) if cuts else 1.0
    entries = jax.random.normal(key, dims, jnp.float32) * scale * level
    return jnp.minimum(jnp.maximum(entries, -limit), limit).astype(kind)


def setup_inputs(seed: int = 0) -> dict:
    keys = jax.random.split(jax.random.key(seed), 7)
    out_gate = bell_draw(keys[0], (SEQUENCE_TOKENS, CHANNELS), 1.0, 6.0, ((0, 64), (1, 4)))
    in_gate = draw_in_gate(jax.random.fold_in(keys[6], 71), 0)
    values = draw_values(jax.random.fold_in(keys[6], 71), 0)
    filter_param = draw_filter_param(jax.random.fold_in(keys[6], 71), 0)
    out_weight = bell_draw(keys[4], (CHANNELS, DOUT), CHANNELS ** -0.5, 0.125, ((0, 4),))
    out_cotangent = bell_draw(keys[5], (SEQUENCE_TOKENS, DOUT), 1.0, 6.0, ((0, 256),))
    return dict(out_gate=out_gate, in_gate=in_gate, values=values, filter_param=filter_param, out_weight=out_weight, out_cotangent=out_cotangent)


def reference(out_gate, in_gate, values, filter_param, out_weight, out_cotangent):
    block_cols = min(256, CHANNELS)
    block_count = CHANNELS // block_cols
    scale_factor = 1.0 / math.sqrt(SEQUENCE_TOKENS)

    def to_blocks(array):
        return array.reshape(SEQUENCE_TOKENS, block_count, block_cols).transpose(1, 0, 2)

    def from_blocks(array):
        return array.transpose(1, 0, 2).reshape(SEQUENCE_TOKENS, CHANNELS)

    def per_block(pieces):
        gate_after, gate_before, value_cols, filter_cols, weight_rows = pieces
        gate_after = gate_after.astype(jnp.float32)
        gate_before = gate_before.astype(jnp.float32)
        value_cols = value_cols.astype(jnp.float32)
        source = gate_before * value_cols
        kernel = filter_cols.astype(jnp.float32) * scale_factor
        source_spec = jnp.fft.rfft(source, axis=0)
        kernel_spec = jnp.fft.rfft(kernel, axis=0)
        conv = jnp.fft.irfft(source_spec * kernel_spec, n=SEQUENCE_TOKENS, axis=0)
        gated = (gate_after * conv).astype(jnp.bfloat16)
        d_gated = jnp.dot(out_cotangent, weight_rows.T, preferred_element_type=jnp.float32)
        d_after = d_gated * conv
        d_conv = d_gated * gate_after
        conv_spec = jnp.fft.rfft(d_conv, axis=0)
        d_source = jnp.fft.irfft(jnp.conj(kernel_spec) * conv_spec, n=SEQUENCE_TOKENS, axis=0)
        d_kernel = jnp.fft.irfft(jnp.conj(source_spec) * conv_spec, n=SEQUENCE_TOKENS, axis=0)
        d_before = d_source * value_cols
        d_value = d_source * gate_before
        d_filter_cols = d_kernel * scale_factor
        return (gated, d_after, d_before, d_value, d_filter_cols)
    results = lax.map(per_block, (to_blocks(out_gate), to_blocks(in_gate), to_blocks(values), to_blocks(filter_param), out_weight.reshape(block_count, block_cols, DOUT)))
    gated = from_blocks(results[0])
    output = jnp.dot(gated, out_weight, preferred_element_type=jnp.float32).astype(jnp.bfloat16)
    return (output, from_blocks(results[1]), from_blocks(results[2]), from_blocks(results[3]), from_blocks(results[4]))
```

```python
import functools
import math

import jax
import jax.numpy as jnp
import ml_dtypes
import numpy as np
from jax import lax
from jax.experimental import pallas as pl
from jax.experimental.pallas import tpu as pltpu
from jax.sharding import PartitionSpec as P

MESH = pl.DeviceIdType.MESH
F32 = jnp.float32
BF16 = jnp.bfloat16
GROUP = 8
K_SLOT, S_SLOT, D_SLOT, C_SLOT, DS_SLOT, DK_SLOT = range(6)


def split_table(table):
    high = table.astype(np.float32).astype(ml_dtypes.bfloat16)
    low = (table - high.astype(np.float64)).astype(np.float32).astype(ml_dtypes.bfloat16)
    return high, low


def make_tables(parts, rows):
    total = parts * rows
    kept = parts // 2 + 1
    padded = kept + kept % 2
    k1 = np.arange(padded)
    shard = np.arange(parts)
    pos = np.arange(rows)
    eye = np.eye(GROUP)
    angle = 2.0 * np.pi * ((k1[:, None] * shard[None, :]) % parts) / parts
    across = np.concatenate([np.kron(np.cos(angle), eye), np.kron(-np.sin(angle), eye)], 0)
    across_table = np.concatenate(split_table(across), 0)
    weight = np.where((k1 == 0) | (k1 == parts // 2), 1.0, 2.0) * (k1 < kept)
    factor = weight / (total * math.sqrt(total))
    back = np.concatenate([np.kron((np.cos(angle) * factor[:, None]).T, eye), np.kron((np.sin(angle) * factor[:, None]).T, eye)], 1)
    back_high, back_low = split_table(back)
    back_table = np.concatenate([back_high, back_high, back_low], 1)
    square = 2.0 * np.pi * ((pos[:, None] * pos[None, :]) % rows) / rows
    within = np.block([[np.cos(square), -np.sin(square)], [np.sin(square), np.cos(square)]])
    within_high, within_low = split_table(within)
    turn = 2.0 * np.pi * (k1[:, None] * pos[None, :]) / total
    turn_re = np.repeat(np.cos(turn), GROUP, 0).astype(np.float32)
    turn_im = np.repeat(-np.sin(turn), GROUP, 0).astype(np.float32)
    return across_table, within_high, within_low, back_table, turn_re, turn_im


def split_value(value):
    high = value.astype(BF16)
    return high, (value - high.astype(F32)).astype(BF16)


def kernel(
    og_ref, ig_ref, val_ref, fil_ref, w_ref, cot_ref,
    across_ref, within_hi_ref, within_lo_ref, back_ref, turn_re_ref, turn_im_ref,
    out_ref, d_og_ref, d_ig_ref, d_val_ref, d_fil_ref,
    snd, rcv, cots, d_gated, time_buf, gated, chan_buf, lhs, spec, stack,
    core_snd, core_rcv, y_snd, y_rcv, total_buf,
    snd_sem, rcv_sem, cot_snd_sem, cot_rcv_sem, red_snd_sem, red_rcv_sem,
):
    parts = lax.axis_size("seq")
    me, ch = lax.axis_index("seq"), lax.axis_index("chan")
    core, high = lax.rem(ch, 2), ch // 2
    core_peer = high * 2 + (1 - core)
    y_peer = (1 - high) * 2 + core
    far_peer = (1 - high) * 2 + (1 - core)
    rows, width = val_ref.shape
    half = rows // 2
    tile = min(128, width)
    tiles = width // tile
    groups = tile // GROUP
    msg = 2 * GROUP
    nk = turn_re_ref.shape[0]
    blk, dout = cot_ref.shape

    barrier = pltpu.get_barrier_semaphore()

    def greet(d, _):
        pl.semaphore_signal(barrier, inc=1, device_id=(lax.rem(me + d, parts), ch), device_id_type=MESH)
        return 0

    lax.fori_loop(1, parts, greet, 0)
    pl.semaphore_signal(barrier, inc=1, device_id=(me, core_peer), device_id_type=MESH)
    pl.semaphore_signal(barrier, inc=1, device_id=(me, y_peer), device_id_type=MESH)

    def message(p):
        return pl.ds(pl.multiple_of(p * msg, msg), msg)

    def send(slot):
        def go(i, _):
            p = lax.rem(me + lax.rem(i * 37, parts), parts)
            pltpu.make_async_remote_copy(
                src_ref=snd.at[slot, message(p)],
                dst_ref=rcv.at[slot, message(me)],
                send_sem=snd_sem.at[slot],
                recv_sem=rcv_sem.at[slot],
                device_id=(p, ch),
                device_id_type=MESH,
            ).start()
            return 0

        lax.fori_loop(1, parts, go, 0)
        rcv[slot, message(me)] = snd[slot, message(me)]

    def await_bytes(slot, sem):
        ref = rcv.at[slot, pl.ds(0, (parts - 1) * msg)]
        pltpu.make_async_copy(ref, ref, sem.at[slot]).wait()

    def to_messages(slot, first, second, row):
        n = first.shape[0] // GROUP
        both = jnp.concatenate([first.reshape(n, GROUP, half), second.reshape(n, GROUP, half)], 1)
        snd[slot, pl.ds(row, n * msg)] = both.reshape(n * msg, half).astype(BF16)

    def from_messages(slot, row, n):
        both = rcv[slot, pl.ds(row, n * msg)].astype(F32).reshape(n, msg, half)
        return both[:, :GROUP].reshape(n * GROUP, half), both[:, GROUP:].reshape(n * GROUP, half)

    def pack(slot, load):
        def go(t, _):
            cols = pl.ds(pl.multiple_of(t * tile, tile), tile)
            first, second = (load(pl.ds(h * half, half), cols).T for h in range(2))
            to_messages(slot, first, second, pl.multiple_of(t * groups * msg, groups * msg))
            return 0

        lax.fori_loop(0, tiles, go, 0)

    def unpack(slot, store):
        def go(t, _):
            cols = pl.ds(pl.multiple_of(t * tile, tile), tile)
            halves = from_messages(slot, pl.multiple_of(t * groups * msg, groups * msg), groups)
            for h in range(2):
                store(pl.ds(h * half, half), cols, halves[h].T)
            return 0

        lax.fori_loop(0, tiles, go, 0)

    def turn(real, imag, cols):
        a, b = turn_re_ref[:, cols], turn_im_ref[:, cols]
        return real * a - imag * b, real * b + imag * a

    def put_lhs(real, imag, cols, cols_imag):
        for value, at in ((real, cols), (imag, cols_imag)):
            hi, lo = split_value(value)
            lhs[:nk, at] = hi
            lhs[nk:, at] = lo

    def halves_of(h):
        return (
            pl.ds(pl.multiple_of(h * half, half), half),
            pl.ds(pl.multiple_of(rows + h * half, half), half),
        )

    def within(dst):
        def go(j, _):
            cols = pl.ds(pl.multiple_of(j * half, half), half)
            both = jnp.dot(lhs[...], within_hi_ref[:, cols], preferred_element_type=F32)
            rest = jnp.dot(lhs[:nk], within_lo_ref[:, cols], preferred_element_type=F32)
            spec[dst, :, cols] = both[:nk] + both[nk:] + rest
            return 0

        lax.fori_loop(0, 4, go, 0)

    def forward(slot, dst):
        step = min(16, parts)

        def regroup(i, _):
            first, second = from_messages(slot, pl.multiple_of(i * step * msg, step * msg), step)
            at = pl.ds(pl.multiple_of(i * step * GROUP, step * GROUP), step * GROUP)
            chan_buf[at, :half] = first.astype(BF16)
            chan_buf[at, half:] = second.astype(BF16)
            return 0

        lax.fori_loop(0, parts // step, regroup, 0)

        def go(h, _):
            cols, cols_imag = halves_of(h)
            y = jnp.dot(across_ref[...], chan_buf[:, cols], preferred_element_type=F32)
            y = y[: 2 * nk] + y[2 * nk :]
            real, imag = turn(y[:nk], y[nk:], cols)
            put_lhs(real, imag, cols, cols_imag)
            return 0

        lax.fori_loop(0, 2, go, 0)
        within(dst)

    def inverse(slot, product):
        def fill(h, _):
            cols, cols_imag = halves_of(h)
            real, imag = product(cols, cols_imag)
            put_lhs(real, imag, cols, cols_imag)
            return 0

        lax.fori_loop(0, 2, fill, 0)
        within(3)

        def go(h, _):
            cols, cols_imag = halves_of(h)
            real, imag = turn(spec[3, :, cols], spec[3, :, cols_imag], cols)
            for i, value in enumerate((real, imag)):
                hi, lo = split_value(value)
                stack[i * nk : (i + 1) * nk, cols] = hi
                stack[(2 + i) * nk : (3 + i) * nk, cols] = lo
                stack[(4 + i) * nk : (5 + i) * nk, cols] = hi
            time_buf[:, cols] = jnp.dot(back_ref[...], stack[:, cols], preferred_element_type=F32)
            return 0

        lax.fori_loop(0, 2, go, 0)
        step = min(16, parts)

        def regroup(i, _):
            at = pl.ds(pl.multiple_of(i * step * GROUP, step * GROUP), step * GROUP)
            to_messages(slot, time_buf[at, :half], time_buf[at, half:], pl.multiple_of(i * step * msg, step * msg))
            return 0

        lax.fori_loop(0, parts // step, regroup, 0)
        send(slot)

    pack(K_SLOT, lambda r, c: fil_ref[r, c].astype(F32))
    pl.semaphore_wait(barrier, parts + 1)

    def to_chan(i, src, dst, peer, snd_sems, rcv_sems):
        return pltpu.make_async_remote_copy(
            src_ref=src, dst_ref=dst, send_sem=snd_sems.at[i], recv_sem=rcv_sems.at[i],
            device_id=(me, peer), device_id_type=MESH,
        )

    cot_y = to_chan(0, cot_ref, cots.at[ch], y_peer, cot_snd_sem, cot_rcv_sem)
    cot_core = to_chan(1, cot_ref, cots.at[ch], core_peer, cot_snd_sem, cot_rcv_sem)
    cot_y.start()
    cot_core.start()
    send(K_SLOT)
    pack(S_SLOT, lambda r, c: ig_ref[r, c].astype(F32) * val_ref[r, c].astype(F32))
    send(S_SLOT)

    def d_block(block_ref, b):
        at = pl.ds(pl.multiple_of(b * blk, blk), blk)
        d = lax.dot_general(block_ref[...], w_ref[...], (((1,), (1,)), ((), ())), preferred_element_type=F32)
        d_gated[at] = d
        time_buf[at] = d * og_ref[at].astype(F32)

    d_block(cot_ref, ch)
    cot_y.wait_recv()
    cot_far = to_chan(2, cots.at[y_peer], cots.at[y_peer], core_peer, cot_snd_sem, cot_rcv_sem)
    cot_far.start()
    d_block(cots.at[y_peer], y_peer)
    cot_core.wait_recv()
    d_block(cots.at[core_peer], core_peer)
    cot_far.wait_recv()
    d_block(cots.at[far_peer], far_peer)
    pack(D_SLOT, lambda r, c: time_buf[r, c])
    send(D_SLOT)

    await_bytes(K_SLOT, rcv_sem)
    forward(K_SLOT, 0)
    await_bytes(S_SLOT, rcv_sem)
    forward(S_SLOT, 1)

    def conv_product(cols, cols_imag):
        a, b = spec[0, :, cols], spec[0, :, cols_imag]
        c, d = spec[1, :, cols], spec[1, :, cols_imag]
        return a * c - b * d, -(a * d + b * c)

    inverse(C_SLOT, conv_product)
    await_bytes(D_SLOT, rcv_sem)
    forward(D_SLOT, 2)

    def correlation(which):
        def product(cols, cols_imag):
            a, b = spec[which, :, cols], spec[which, :, cols_imag]
            c, d = spec[2, :, cols], spec[2, :, cols_imag]
            return a * c + b * d, b * c - a * d

        return product

    inverse(DS_SLOT, correlation(0))
    inverse(DK_SLOT, correlation(1))

    await_bytes(C_SLOT, rcv_sem)

    def use_conv(r, c, conv):
        gated[r, c] = (og_ref[r, c].astype(F32) * conv).astype(BF16)
        d_og_ref[r, c] = d_gated[r, c] * conv

    unpack(C_SLOT, use_conv)
    out_tile = min(512, dout)

    def project(of_core, store):
        for j in range(2):
            at = pl.ds(pl.multiple_of((2 * j + of_core) * blk, blk), blk)

            def go(n, _, j=j, at=at):
                cols = pl.ds(pl.multiple_of(n * out_tile, out_tile), out_tile)
                store(j, cols, jnp.dot(gated[at], w_ref[:, cols], preferred_element_type=F32))
                return 0

            lax.fori_loop(0, dout // out_tile, go, 0)

    def store_peer(j, cols, value):
        core_snd[j, :, cols] = value.astype(BF16)

    def store_mine(j, cols, value):
        total_buf[j, :, cols] = value

    project(1 - core, store_peer)
    red_core = to_chan(0, core_snd, core_rcv, core_peer, red_snd_sem, red_rcv_sem)
    red_core.start()
    project(core, store_mine)
    red_core.wait_recv()
    y_snd[...] = (total_buf[1 - high] + core_rcv[1 - high].astype(F32)).astype(BF16)
    red_y = to_chan(1, y_snd, y_rcv, y_peer, red_snd_sem, red_rcv_sem)
    red_y.start()
    total_buf[high] = total_buf[high] + core_rcv[high].astype(F32)
    red_y.wait_recv()
    out_ref[...] = (total_buf[high] + y_rcv[...].astype(F32)).astype(BF16)

    await_bytes(DS_SLOT, rcv_sem)

    def use_source(r, c, grad):
        d_ig_ref[r, c] = grad * val_ref[r, c].astype(F32)
        d_val_ref[r, c] = grad * ig_ref[r, c].astype(F32)

    unpack(DS_SLOT, use_source)
    await_bytes(DK_SLOT, rcv_sem)

    def use_kernel(r, c, grad):
        d_fil_ref[r, c] = grad

    unpack(DK_SLOT, use_kernel)

    for slot in range(6):
        await_bytes(slot, snd_sem)
    for copy in (cot_y, cot_core, cot_far, red_core, red_y):
        copy.wait_send()


def on_device(out_gate, in_gate, values, filter_param, out_weight, out_cotangent):
    rows, width = values.shape
    parts = lax.axis_size("seq")
    blk, dout = out_cotangent.shape
    tables = make_tables(parts, rows)
    nk = tables[4].shape[0]
    msgs = (parts * 2 * GROUP, rows // 2)
    vmem = pl.BlockSpec(memory_space=pltpu.VMEM)
    grad = jax.ShapeDtypeStruct((rows, width), F32)
    return pl.pallas_call(
        kernel,
        out_shape=(jax.ShapeDtypeStruct((blk, dout), BF16), grad, grad, grad, grad),
        in_specs=[vmem] * 12,
        out_specs=(vmem,) * 5,
        scratch_shapes=[
            pltpu.VMEM((6, *msgs), BF16),
            pltpu.VMEM((6, *msgs), BF16),
            pltpu.VMEM((4, blk, dout), BF16),
            pltpu.VMEM((rows, width), F32),
            pltpu.VMEM((rows, width), F32),
            pltpu.VMEM((rows, width), BF16),
            pltpu.VMEM((parts * GROUP, rows), BF16),
            pltpu.VMEM((2 * nk, 2 * rows), BF16),
            pltpu.VMEM((4, nk, 2 * rows), F32),
            pltpu.VMEM((6 * nk, rows), BF16),
            pltpu.VMEM((2, blk, dout), BF16),
            pltpu.VMEM((2, blk, dout), BF16),
            pltpu.VMEM((blk, dout), BF16),
            pltpu.VMEM((blk, dout), BF16),
            pltpu.VMEM((2, blk, dout), F32),
            pltpu.SemaphoreType.DMA((6,)),
            pltpu.SemaphoreType.DMA((6,)),
            pltpu.SemaphoreType.DMA((3,)),
            pltpu.SemaphoreType.DMA((3,)),
            pltpu.SemaphoreType.DMA((2,)),
            pltpu.SemaphoreType.DMA((2,)),
        ],
        compiler_params=pltpu.CompilerParams(collective_id=0, has_side_effects=True, vmem_limit_bytes=60 * 2**20),
    )(out_gate, in_gate, values, filter_param, out_weight, out_cotangent, *tables)


def solution(mesh):
    return jax.shard_map(
        on_device,
        mesh=mesh,
        in_specs=(
            P("seq", "chan"),
            P("seq", "chan"),
            P("seq", "chan"),
            P("seq", "chan"),
            P("chan", None),
            P(("seq", "chan"), None),
        ),
        out_specs=(
            P(("seq", "chan"), None),
            P("seq", "chan"),
            P("seq", "chan"),
            P("seq", "chan"),
            P("seq", "chan"),
        ),
        check_vma=False,
    )
```

```python
import functools
import math

import jax
import jax.numpy as jnp
import ml_dtypes
import numpy as np
from jax import lax
from jax.experimental import pallas as pl
from jax.experimental.pallas import tpu as pltpu
from jax.sharding import PartitionSpec as P

MESH = pl.DeviceIdType.MESH
F32 = jnp.float32
BF16 = jnp.bfloat16
GROUP = 8
TILE = 128
K_SLOT, S_SLOT, D_SLOT, C_SLOT, DS_SLOT, DK_SLOT = range(6)


def split_table(table):
    high = table.astype(np.float32).astype(ml_dtypes.bfloat16)
    low = (table - high.astype(np.float64)).astype(np.float32).astype(ml_dtypes.bfloat16)
    return high, low


def make_tables(parts, rows):
    total = parts * rows
    kept = parts // 2 + 1
    padded = kept + kept % 2
    k1 = np.arange(padded)
    shard = np.arange(parts)
    pos = np.arange(rows)
    eye = np.eye(GROUP)
    angle = 2.0 * np.pi * ((k1[:, None] * shard[None, :]) % parts) / parts
    across = np.concatenate([np.kron(np.cos(angle), eye), np.kron(-np.sin(angle), eye)], 0)
    across_table = np.concatenate(split_table(across), 0)
    weight = np.where((k1 == 0) | (k1 == parts // 2), 1.0, 2.0) * (k1 < kept)
    factor = weight / (total * math.sqrt(total))
    back = np.concatenate([np.kron((np.cos(angle) * factor[:, None]).T, eye), np.kron((np.sin(angle) * factor[:, None]).T, eye)], 1)
    back_high, back_low = split_table(back)
    back_table = np.concatenate([back_high, back_high, back_low], 1)
    square = 2.0 * np.pi * ((pos[:, None] * pos[None, :]) % rows) / rows
    within = np.block([[np.cos(square), -np.sin(square)], [np.sin(square), np.cos(square)]])
    within_high, within_low = split_table(within)
    turn = 2.0 * np.pi * (k1[:, None] * pos[None, :]) / total
    turn_re = np.repeat(np.cos(turn), GROUP, 0).astype(np.float32)
    turn_im = np.repeat(-np.sin(turn), GROUP, 0).astype(np.float32)
    return across_table, within_high, within_low, back_table, turn_re, turn_im


def split_value(value):
    high = value.astype(BF16)
    return high, (value - high.astype(F32)).astype(BF16)


def kernel(
    og_hbm, ig_hbm, val_hbm, fil_hbm, w_hbm, cot_hbm,
    across_hbm, within_hi_hbm, within_lo_hbm, back_hbm, turn_re_hbm, turn_im_hbm,
    out_hbm, d_og_hbm, ds_hbm, dk_hbm,
    og_ref, ig_ref, val_ref, fil_ref, w_ref,
    across_ref, within_hi_ref, within_lo_ref, back_ref, turn_re_ref, turn_im_ref,
    snd, rcv, cots, d_gated, time_buf, gated, d_og_buf, chan_buf, lhs, spec, stack,
    core_snd, core_rcv, y_snd, y_rcv, total_buf, out_buf,
    load_sem, store_sem, snd_sem, rcv_sem, cot_snd_sem, cot_rcv_sem, red_snd_sem, red_rcv_sem,
):
    parts = lax.axis_size("seq")
    me, ch = lax.axis_index("seq"), lax.axis_index("chan")
    core, high = lax.rem(ch, 2), ch // 2
    core_peer = high * 2 + (1 - core)
    y_peer = (1 - high) * 2 + core
    far_peer = (1 - high) * 2 + (1 - core)
    rows, width = val_ref.shape
    half = rows // 2
    tile = min(TILE, width)
    tiles = width // tile
    groups = tile // GROUP
    msg = 2 * GROUP
    nk = turn_re_ref.shape[0]
    _, blk, dout = cots.shape
    my_tile, my_group = lax.rem(me, tiles), me // tiles
    my_slot = my_tile * groups + my_group

    loads = {}
    for i, (name, src, dst) in enumerate(
        (
            ("cot", cot_hbm, cots.at[ch]),
            ("fil", fil_hbm, fil_ref),
            ("ig", ig_hbm, ig_ref),
            ("val", val_hbm, val_ref),
            ("w", w_hbm, w_ref),
            ("og", og_hbm, og_ref),
            ("across", across_hbm, across_ref),
            ("turn_re", turn_re_hbm, turn_re_ref),
            ("turn_im", turn_im_hbm, turn_im_ref),
            ("within_hi", within_hi_hbm, within_hi_ref),
            ("within_lo", within_lo_hbm, within_lo_ref),
            ("back", back_hbm, back_ref),
        )
    ):
        loads[name] = pltpu.make_async_copy(src, dst, load_sem.at[i])
        loads[name].start()

    def loaded(*names):
        for name in names:
            loads[name].wait()

    barrier = pltpu.get_barrier_semaphore()

    def greet(d, _):
        pl.semaphore_signal(barrier, inc=1, device_id=(lax.rem(me + d, parts), ch), device_id_type=MESH)
        return 0

    pl.semaphore_signal(barrier, inc=1, device_id=(me, core_peer), device_id_type=MESH)
    pl.semaphore_signal(barrier, inc=1, device_id=(me, y_peer), device_id_type=MESH)
    lax.fori_loop(1, parts, greet, 0)

    def message(p):
        return pl.ds(pl.multiple_of(p * msg, msg), msg)

    def send_one(slot, src_slot, dst, p):
        pltpu.make_async_remote_copy(
            src_ref=snd.at[slot, message(src_slot)],
            dst_ref=dst,
            send_sem=snd_sem.at[slot],
            recv_sem=rcv_sem.at[slot],
            device_id=(p, ch),
            device_id_type=MESH,
        ).start()

    def send_back(slot, dst):
        def go(i, _):
            p = lax.rem(me + lax.rem(i * 37, parts), parts)
            send_one(slot, p, dst, p)
            return 0

        lax.fori_loop(1, parts, go, 0)

    def await_bytes(ref, sem):
        ref = ref.at[pl.ds(0, (parts - 1) * msg)]
        pltpu.make_async_copy(ref, ref, sem).wait()

    def arrived(slot):
        await_bytes(rcv.at[slot], rcv_sem.at[slot])

    def to_messages(slot, first, second, row):
        n = first.shape[0] // GROUP
        both = jnp.concatenate([first.reshape(n, GROUP, half), second.reshape(n, GROUP, half)], 1)
        snd[slot, pl.ds(row, n * msg)] = both.reshape(n * msg, half).astype(BF16)

    def send_tile(slot, load, u):
        t = lax.rem(my_tile + u, tiles)
        cols = pl.ds(pl.multiple_of(t * tile, tile), tile)
        first, second = (load(pl.ds(h * half, half), cols).T for h in range(2))
        to_messages(slot, first, second, pl.multiple_of(t * groups * msg, groups * msg))

        def go(i, _):
            j = lax.rem(my_group + i, groups)
            send_one(slot, t * groups + j, rcv.at[slot, message(me)], j * tiles + t)
            return 0

        lax.fori_loop(jnp.maximum(1 - u, 0), groups, go, 0)

    def send_tiles(slot, load, start, stop):
        def go(u, _):
            send_tile(slot, load, u)
            return 0

        lax.fori_loop(start, stop, go, 0)
        if start == 0:
            rcv[slot, message(me)] = snd[slot, message(my_slot)]

    def turn(real, imag, cols):
        a, b = turn_re_ref[:, cols], turn_im_ref[:, cols]
        return real * a - imag * b, real * b + imag * a

    def put_lhs(real, imag, cols, cols_imag):
        for value, at in ((real, cols), (imag, cols_imag)):
            hi, lo = split_value(value)
            lhs[:nk, at] = hi
            lhs[nk:, at] = lo

    def halves_of(h):
        return (
            pl.ds(pl.multiple_of(h * half, half), half),
            pl.ds(pl.multiple_of(rows + h * half, half), half),
        )

    def within(dst):
        def go(j, _):
            cols = pl.ds(pl.multiple_of(j * half, half), half)
            both = jnp.dot(lhs[...], within_hi_ref[:, cols], preferred_element_type=F32)
            rest = jnp.dot(lhs[:nk], within_lo_ref[:, cols], preferred_element_type=F32)
            spec[dst, :, cols] = both[:nk] + both[nk:] + rest
            return 0

        lax.fori_loop(0, 4, go, 0)

    step = min(16, parts)

    def forward(slot, dst):
        def regroup(i, _):
            both = rcv[slot, pl.ds(pl.multiple_of(i * step * msg, step * msg), step * msg)]
            both = both.astype(F32).reshape(step, msg, half)
            at = pl.ds(pl.multiple_of(i * step * GROUP, step * GROUP), step * GROUP)
            chan_buf[at, :half] = both[:, :GROUP].reshape(step * GROUP, half).astype(BF16)
            chan_buf[at, half:] = both[:, GROUP:].reshape(step * GROUP, half).astype(BF16)
            return 0

        lax.fori_loop(0, parts // step, regroup, 0)

        def go(h, _):
            cols, cols_imag = halves_of(h)
            y = jnp.dot(across_ref[...], chan_buf[:, cols], preferred_element_type=F32)
            y = y[: 2 * nk] + y[2 * nk :]
            real, imag = turn(y[:nk], y[nk:], cols)
            put_lhs(real, imag, cols, cols_imag)
            return 0

        lax.fori_loop(0, 2, go, 0)
        within(dst)

    def inverse(slot, product):
        def fill(h, _):
            cols, cols_imag = halves_of(h)
            real, imag = product(cols, cols_imag)
            put_lhs(real, imag, cols, cols_imag)
            return 0

        lax.fori_loop(0, 2, fill, 0)
        within(3)

        def go(h, _):
            cols, cols_imag = halves_of(h)
            real, imag = turn(spec[3, :, cols], spec[3, :, cols_imag], cols)
            for i, value in enumerate((real, imag)):
                hi, lo = split_value(value)
                stack[i * nk : (i + 1) * nk, cols] = hi
                stack[(2 + i) * nk : (3 + i) * nk, cols] = lo
                stack[(4 + i) * nk : (5 + i) * nk, cols] = hi
            time_buf[:, cols] = jnp.dot(back_ref[...], stack[:, cols], preferred_element_type=F32)
            return 0

        lax.fori_loop(0, 2, go, 0)

        def regroup(i, _):
            at = pl.ds(pl.multiple_of(i * step * GROUP, step * GROUP), step * GROUP)
            to_messages(slot, time_buf[at, :half], time_buf[at, half:], pl.multiple_of(i * step * msg, step * msg))
            return 0

        lax.fori_loop(0, parts // step, regroup, 0)

    def to_chan(i, src, dst, peer, snd_sems, rcv_sems):
        return pltpu.make_async_remote_copy(
            src_ref=src, dst_ref=dst, send_sem=snd_sems.at[i], recv_sem=rcv_sems.at[i],
            device_id=(me, peer), device_id_type=MESH,
        )

    def cot_copy(i, owner, h, peer):
        ref = cots.at[owner, pl.ds(h * (blk // 2), blk // 2)]
        return to_chan(i, ref, ref, peer, cot_snd_sem, cot_rcv_sem)

    cot_y = [cot_copy(h, ch, h, y_peer) for h in range(2)]
    cot_core = to_chan(2, cots.at[ch], cots.at[ch], core_peer, cot_snd_sem, cot_rcv_sem)
    cot_far = [cot_copy(3 + h, y_peer, h, core_peer) for h in range(2)]

    loaded("cot", "fil")
    pl.semaphore_wait(barrier, parts + 1)
    cot_y[0].start()
    cot_y[1].start()
    cot_core.start()
    send_tiles(K_SLOT, lambda r, c: fil_ref[r, c].astype(F32), 0, tiles)
    loaded("ig", "val")

    def source(r, c):
        return ig_ref[r, c].astype(F32) * val_ref[r, c].astype(F32)

    send_tiles(S_SLOT, source, 0, tiles // 2)
    loaded("w", "og")

    def d_block(b):
        at = pl.ds(pl.multiple_of(b * blk, blk), blk)
        d = lax.dot_general(cots[b], w_ref[...], (((1,), (1,)), ((), ())), preferred_element_type=F32)
        d_gated[at] = d
        time_buf[at] = d * og_ref[at].astype(F32)

    d_block(ch)
    for h in range(2):
        cot_y[h].wait_recv()
        cot_far[h].start()
    send_tiles(S_SLOT, source, tiles // 2, tiles)
    d_block(y_peer)
    cot_core.wait_recv()
    d_block(core_peer)
    cot_far[0].wait_recv()
    cot_far[1].wait_recv()
    d_block(far_peer)
    send_tiles(D_SLOT, lambda r, c: time_buf[r, c], 0, tiles)

    loaded("across", "turn_re", "turn_im", "within_hi", "within_lo", "back")
    arrived(K_SLOT)
    forward(K_SLOT, 0)
    arrived(S_SLOT)
    forward(S_SLOT, 1)

    def conv_product(cols, cols_imag):
        a, b = spec[0, :, cols], spec[0, :, cols_imag]
        c, d = spec[1, :, cols], spec[1, :, cols_imag]
        return a * c - b * d, -(a * d + b * c)

    inverse(C_SLOT, conv_product)
    send_back(C_SLOT, rcv.at[C_SLOT, message(my_slot)])
    rcv[C_SLOT, message(my_slot)] = snd[C_SLOT, message(me)]
    arrived(D_SLOT)
    forward(D_SLOT, 2)

    def correlation(which):
        def product(cols, cols_imag):
            a, b = spec[which, :, cols], spec[which, :, cols_imag]
            c, d = spec[2, :, cols], spec[2, :, cols_imag]
            return a * c + b * d, b * c - a * d

        return product

    inverse(DS_SLOT, correlation(0))
    send_back(DS_SLOT, ds_hbm.at[message(my_slot)])
    own_ds = pltpu.make_async_copy(snd.at[DS_SLOT, message(me)], ds_hbm.at[message(my_slot)], store_sem.at[0])
    own_ds.start()
    inverse(DK_SLOT, correlation(1))
    own_dk = pltpu.make_async_copy(snd.at[DK_SLOT, message(me)], dk_hbm.at[message(my_slot)], store_sem.at[1])
    own_dk.start()

    arrived(C_SLOT)

    def use_conv(t, _):
        cols = pl.ds(pl.multiple_of(t * tile, tile), tile)
        both = rcv[C_SLOT, pl.ds(pl.multiple_of(t * groups * msg, groups * msg), groups * msg)]
        both = both.astype(F32).reshape(groups, msg, half)
        for h in range(2):
            conv = both[:, h * GROUP : (h + 1) * GROUP].reshape(tile, half).T
            at = pl.ds(h * half, half)
            gated[at, cols] = (og_ref[at, cols].astype(F32) * conv).astype(BF16)
            d_og_buf[at, cols] = d_gated[at, cols] * conv
        return 0

    lax.fori_loop(0, tiles, use_conv, 0)
    d_og_out = pltpu.make_async_copy(d_og_buf, d_og_hbm, store_sem.at[2])
    d_og_out.start()
    out_tile = min(512, dout)

    def project(j, of_core, store):
        at = pl.ds(pl.multiple_of((2 * j + of_core) * blk, blk), blk)

        def go(n, _):
            cols = pl.ds(pl.multiple_of(n * out_tile, out_tile), out_tile)
            store(cols, jnp.dot(gated[at], w_ref[:, cols], preferred_element_type=F32))
            return 0

        lax.fori_loop(0, dout // out_tile, go, 0)

    def store_peer(i):
        def store(cols, value):
            core_snd[i, :, cols] = value.astype(BF16)

        return store

    def store_mine(i):
        def store(cols, value):
            total_buf[i, :, cols] = value

        return store

    red_core = [to_chan(i, core_snd.at[i], core_rcv.at[i], core_peer, red_snd_sem, red_rcv_sem) for i in range(2)]
    red_y = to_chan(2, y_snd, y_rcv, y_peer, red_snd_sem, red_rcv_sem)
    project(1 - high, 1 - core, store_peer(0))
    red_core[0].start()
    project(1 - high, core, store_mine(0))
    red_core[0].wait_recv()
    y_snd[...] = (total_buf[0] + core_rcv[0].astype(F32)).astype(BF16)
    red_y.start()
    project(high, 1 - core, store_peer(1))
    red_core[1].start()
    send_back(DK_SLOT, dk_hbm.at[message(my_slot)])
    project(high, core, store_mine(1))
    red_core[1].wait_recv()
    total_buf[1] = total_buf[1] + core_rcv[1].astype(F32)
    red_y.wait_recv()
    out_buf[...] = (total_buf[1] + y_rcv[...].astype(F32)).astype(BF16)
    out_out = pltpu.make_async_copy(out_buf, out_hbm, store_sem.at[3])
    out_out.start()

    await_bytes(ds_hbm, rcv_sem.at[DS_SLOT])
    for slot in range(6):
        await_bytes(snd.at[slot], snd_sem.at[slot])
    for copy in (*cot_y, cot_core, *cot_far, *red_core, red_y):
        copy.wait_send()
    for copy in (own_ds, own_dk, d_og_out, out_out):
        copy.wait()
    await_bytes(dk_hbm, rcv_sem.at[DK_SLOT])


def finish(ig_ref, val_ref, ds_ref, dk_ref, d_og_in, out_in, d_ig_ref, d_val_ref, d_fil_ref, d_og_ref, out_ref):
    rows, tile = val_ref.shape
    half = rows // 2
    groups = tile // GROUP

    def positions(ref, h):
        both = ref[...].astype(F32).reshape(groups, 2 * GROUP, half)
        return both[:, h * GROUP : (h + 1) * GROUP].reshape(tile, half).T

    for h in range(2):
        at = pl.ds(h * half, half)
        grad = positions(ds_ref, h)
        d_ig_ref[at] = grad * val_ref[at].astype(F32)
        d_val_ref[at] = grad * ig_ref[at].astype(F32)
        d_fil_ref[at] = positions(dk_ref, h)
    d_og_ref[...] = d_og_in[...]
    out_ref[...] = out_in[...]


def on_device(out_gate, in_gate, values, filter_param, out_weight, out_cotangent):
    rows, width = values.shape
    parts = lax.axis_size("seq")
    blk, dout = out_cotangent.shape
    tables = make_tables(parts, rows)
    nk = tables[4].shape[0]
    msgs = (parts * 2 * GROUP, rows // 2)
    tile = min(TILE, width)
    tiles = width // tile
    operands = (out_gate, in_gate, values, filter_param, out_weight, out_cotangent, *tables)
    grad = jax.ShapeDtypeStruct((rows, width), F32)
    block_out = jax.ShapeDtypeStruct((blk, dout), BF16)
    raw = jax.ShapeDtypeStruct(msgs, BF16)
    anywhere = pl.BlockSpec(memory_space=pl.ANY)
    output, d_og, ds_raw, dk_raw = pl.pallas_call(
        kernel,
        out_shape=(block_out, grad, raw, raw),
        in_specs=[anywhere] * 12,
        out_specs=(anywhere,) * 4,
        scratch_shapes=[
            *(pltpu.VMEM(x.shape, x.dtype) for i, x in enumerate(operands) if i != 5),
            pltpu.VMEM((6, *msgs), BF16),
            pltpu.VMEM((4, *msgs), BF16),
            pltpu.VMEM((4, blk, dout), BF16),
            pltpu.VMEM((rows, width), F32),
            pltpu.VMEM((rows, width), F32),
            pltpu.VMEM((rows, width), BF16),
            pltpu.VMEM((rows, width), F32),
            pltpu.VMEM((parts * GROUP, rows), BF16),
            pltpu.VMEM((2 * nk, 2 * rows), BF16),
            pltpu.VMEM((4, nk, 2 * rows), F32),
            pltpu.VMEM((6 * nk, rows), BF16),
            pltpu.VMEM((2, blk, dout), BF16),
            pltpu.VMEM((2, blk, dout), BF16),
            pltpu.VMEM((blk, dout), BF16),
            pltpu.VMEM((blk, dout), BF16),
            pltpu.VMEM((2, blk, dout), F32),
            pltpu.VMEM((blk, dout), BF16),
            pltpu.SemaphoreType.DMA((12,)),
            pltpu.SemaphoreType.DMA((4,)),
            pltpu.SemaphoreType.DMA((6,)),
            pltpu.SemaphoreType.DMA((6,)),
            pltpu.SemaphoreType.DMA((5,)),
            pltpu.SemaphoreType.DMA((5,)),
            pltpu.SemaphoreType.DMA((3,)),
            pltpu.SemaphoreType.DMA((3,)),
        ],
        compiler_params=pltpu.CompilerParams(collective_id=0, has_side_effects=True, vmem_limit_bytes=60 * 2**20),
    )(*operands)
    by_channel = pl.BlockSpec((rows, tile), lambda t: (0, t))
    by_row = pl.BlockSpec((msgs[0] // tiles, msgs[1]), lambda t: (t, 0))
    out_rows = pl.BlockSpec((blk // tiles, dout), lambda t: (t, 0))
    d_ig, d_val, d_fil, d_og, output = pl.pallas_call(
        finish,
        grid=(tiles,),
        out_shape=(grad, grad, grad, grad, block_out),
        in_specs=[by_channel, by_channel, by_row, by_row, by_channel, out_rows],
        out_specs=(by_channel, by_channel, by_channel, by_channel, out_rows),
        compiler_params=pltpu.CompilerParams(vmem_limit_bytes=40 * 2**20),
    )(in_gate, values, ds_raw, dk_raw, d_og, output)
    return output, d_og, d_ig, d_val, d_fil


def solution(mesh):
    return jax.shard_map(
        on_device,
        mesh=mesh,
        in_specs=(
            P("seq", "chan"),
            P("seq", "chan"),
            P("seq", "chan"),
            P("seq", "chan"),
            P("chan", None),
            P(("seq", "chan"), None),
        ),
        out_specs=(
            P(("seq", "chan"), None),
            P("seq", "chan"),
            P("seq", "chan"),
            P("seq", "chan"),
            P("seq", "chan"),
        ),
        check_vma=False,
    )
```

```python
import functools
import math

import jax
import jax.numpy as jnp
import ml_dtypes
import numpy as np
from jax import lax
from jax.experimental import pallas as pl
from jax.experimental.pallas import tpu as pltpu
from jax.sharding import PartitionSpec as P

MESH = pl.DeviceIdType.MESH
F32 = jnp.float32
BF16 = jnp.bfloat16
GROUP = 8
TILE = 128
K_SLOT, S_SLOT, D_SLOT, C_SLOT, DS_SLOT, DK_SLOT = range(6)


def split_table(table):
    high = table.astype(np.float32).astype(ml_dtypes.bfloat16)
    low = (table - high.astype(np.float64)).astype(np.float32).astype(ml_dtypes.bfloat16)
    return high, low


def make_tables(parts, rows):
    total = parts * rows
    kept = parts // 2 + 1
    padded = kept + kept % 2
    k1 = np.arange(padded)
    shard = np.arange(parts)
    pos = np.arange(rows)
    eye = np.eye(GROUP)
    angle = 2.0 * np.pi * ((k1[:, None] * shard[None, :]) % parts) / parts
    across = np.concatenate([np.kron(np.cos(angle), eye), np.kron(-np.sin(angle), eye)], 0)
    across_table = np.concatenate(split_table(across), 0)
    weight = np.where((k1 == 0) | (k1 == parts // 2), 1.0, 2.0) * (k1 < kept)
    factor = weight / (total * math.sqrt(total))
    back = np.concatenate([np.kron((np.cos(angle) * factor[:, None]).T, eye), np.kron((np.sin(angle) * factor[:, None]).T, eye)], 1)
    back_high, back_low = split_table(back)
    back_table = np.concatenate([back_high, back_high, back_low], 1)
    square = 2.0 * np.pi * ((pos[:, None] * pos[None, :]) % rows) / rows
    within = np.block([[np.cos(square), -np.sin(square)], [np.sin(square), np.cos(square)]])
    within_high, within_low = split_table(within)
    turn = 2.0 * np.pi * (k1[:, None] * pos[None, :]) / total
    turn_re = np.repeat(np.cos(turn), GROUP, 0).astype(np.float32)
    turn_im = np.repeat(-np.sin(turn), GROUP, 0).astype(np.float32)
    return across_table, within_high, within_low, back_table, turn_re, turn_im


def split_value(value):
    high = value.astype(BF16)
    return high, (value - high.astype(F32)).astype(BF16)


def kernel(
    og_hbm, ig_hbm, val_hbm, fil_hbm, w_hbm, cot_hbm,
    across_hbm, within_hi_hbm, within_lo_hbm, back_hbm, turn_re_hbm, turn_im_hbm,
    out_hbm, d_og_hbm, ds_hbm, dk_hbm,
    og_ref, ig_ref, val_ref, fil_ref, w_ref,
    across_ref, within_hi_ref, within_lo_ref, back_ref, turn_re_ref, turn_im_ref,
    snd, rcv, cots, d_gated, time_buf, gated, d_og_buf, chan_buf, lhs, spec, stack,
    core_snd, core_rcv, y_snd, y_rcv, total_buf, out_buf,
    load_sem, store_sem, snd_sem, rcv_sem, cot_snd_sem, cot_rcv_sem, red_snd_sem, red_rcv_sem,
):
    parts = lax.axis_size("seq")
    me, ch = lax.axis_index("seq"), lax.axis_index("chan")
    core, high = lax.rem(ch, 2), ch // 2
    core_peer = high * 2 + (1 - core)
    y_peer = (1 - high) * 2 + core
    far_peer = (1 - high) * 2 + (1 - core)
    rows, width = val_ref.shape
    half = rows // 2
    tile = min(TILE, width)
    tiles = width // tile
    groups = tile // GROUP
    msg = 2 * GROUP
    nk = turn_re_ref.shape[0]
    _, blk, dout = cots.shape
    my_tile, my_group = lax.rem(me, tiles), me // tiles
    my_slot = my_tile * groups + my_group

    barrier = pltpu.get_barrier_semaphore()

    def greet(d, _):
        pl.semaphore_signal(barrier, inc=1, device_id=(lax.rem(me + d, parts), ch), device_id_type=MESH)
        return 0

    pl.semaphore_signal(barrier, inc=1, device_id=(me, core_peer), device_id_type=MESH)
    pl.semaphore_signal(barrier, inc=1, device_id=(me, y_peer), device_id_type=MESH)
    lax.fori_loop(1, parts, greet, 0)

    loads = {}
    for i, (name, src, dst) in enumerate(
        (
            ("cot", cot_hbm, cots.at[ch]),
            ("fil", fil_hbm, fil_ref),
            ("ig", ig_hbm, ig_ref),
            ("val", val_hbm, val_ref),
            ("w", w_hbm, w_ref),
            ("og", og_hbm, og_ref),
            ("across", across_hbm, across_ref),
            ("turn_re", turn_re_hbm, turn_re_ref),
            ("turn_im", turn_im_hbm, turn_im_ref),
            ("within_hi", within_hi_hbm, within_hi_ref),
            ("within_lo", within_lo_hbm, within_lo_ref),
            ("back", back_hbm, back_ref),
        )
    ):
        loads[name] = pltpu.make_async_copy(src, dst, load_sem.at[i])
        loads[name].start()

    def loaded(*names):
        for name in names:
            loads[name].wait()

    def message(p):
        return pl.ds(pl.multiple_of(p * msg, msg), msg)

    near_parts = parts // 2
    side, place = me // near_parts, lax.rem(me, near_parts)

    def send(slot, crossing, back=False, landing=None):
        landing = rcv.at[slot] if landing is None else landing
        base = (1 - side if crossing else side) * near_parts

        def go(i, _):
            p = base + lax.rem(place + lax.rem(i * 13, near_parts), near_parts)
            by_channel = lax.rem(p, tiles) * groups + p // tiles
            pltpu.make_async_remote_copy(
                src_ref=snd.at[slot, message(p if back else by_channel)],
                dst_ref=landing.at[message(my_slot if back else me)],
                send_sem=snd_sem.at[slot],
                recv_sem=rcv_sem.at[slot],
                device_id=(p, ch),
                device_id_type=MESH,
            ).start()
            return 0

        lax.fori_loop(0 if crossing else 1, near_parts, go, 0)

    def await_bytes(ref, sem):
        ref = ref.at[pl.ds(0, (parts - 1) * msg)]
        pltpu.make_async_copy(ref, ref, sem).wait()

    def arrived(slot):
        await_bytes(rcv.at[slot], rcv_sem.at[slot])

    def to_messages(slot, first, second, row):
        n = first.shape[0] // GROUP
        both = jnp.concatenate([first.reshape(n, GROUP, half), second.reshape(n, GROUP, half)], 1)
        snd[slot, pl.ds(row, n * msg)] = both.reshape(n * msg, half).astype(BF16)

    def pack(slot, load):
        def go(t, _):
            cols = pl.ds(pl.multiple_of(t * tile, tile), tile)
            first, second = (load(pl.ds(h * half, half), cols).T for h in range(2))
            to_messages(slot, first, second, pl.multiple_of(t * groups * msg, groups * msg))
            return 0

        lax.fori_loop(0, tiles, go, 0)
        rcv[slot, message(me)] = snd[slot, message(my_slot)]

    def turn(real, imag, cols):
        a, b = turn_re_ref[:, cols], turn_im_ref[:, cols]
        return real * a - imag * b, real * b + imag * a

    def put_lhs(real, imag, cols, cols_imag):
        for value, at in ((real, cols), (imag, cols_imag)):
            hi, lo = split_value(value)
            lhs[:nk, at] = hi
            lhs[nk:, at] = lo

    def halves_of(h):
        return (
            pl.ds(pl.multiple_of(h * half, half), half),
            pl.ds(pl.multiple_of(rows + h * half, half), half),
        )

    def within(dst):
        def go(j, _):
            cols = pl.ds(pl.multiple_of(j * half, half), half)
            both = jnp.dot(lhs[...], within_hi_ref[:, cols], preferred_element_type=F32)
            rest = jnp.dot(lhs[:nk], within_lo_ref[:, cols], preferred_element_type=F32)
            spec[dst, :, cols] = both[:nk] + both[nk:] + rest
            return 0

        lax.fori_loop(0, 4, go, 0)

    step = min(16, parts)

    def forward(slot, dst):
        def regroup(i, _):
            both = rcv[slot, pl.ds(pl.multiple_of(i * step * msg, step * msg), step * msg)]
            both = both.astype(F32).reshape(step, msg, half)
            at = pl.ds(pl.multiple_of(i * step * GROUP, step * GROUP), step * GROUP)
            chan_buf[at, :half] = both[:, :GROUP].reshape(step * GROUP, half).astype(BF16)
            chan_buf[at, half:] = both[:, GROUP:].reshape(step * GROUP, half).astype(BF16)
            return 0

        lax.fori_loop(0, parts // step, regroup, 0)

        def go(h, _):
            cols, cols_imag = halves_of(h)
            y = jnp.dot(across_ref[...], chan_buf[:, cols], preferred_element_type=F32)
            y = y[: 2 * nk] + y[2 * nk :]
            real, imag = turn(y[:nk], y[nk:], cols)
            put_lhs(real, imag, cols, cols_imag)
            return 0

        lax.fori_loop(0, 2, go, 0)
        within(dst)

    def inverse(slot, product):
        def fill(h, _):
            cols, cols_imag = halves_of(h)
            real, imag = product(cols, cols_imag)
            put_lhs(real, imag, cols, cols_imag)
            return 0

        lax.fori_loop(0, 2, fill, 0)
        within(3)

        def go(h, _):
            cols, cols_imag = halves_of(h)
            real, imag = turn(spec[3, :, cols], spec[3, :, cols_imag], cols)
            for i, value in enumerate((real, imag)):
                hi, lo = split_value(value)
                stack[i * nk : (i + 1) * nk, cols] = hi
                stack[(2 + i) * nk : (3 + i) * nk, cols] = lo
                stack[(4 + i) * nk : (5 + i) * nk, cols] = hi
            time_buf[:, cols] = jnp.dot(back_ref[...], stack[:, cols], preferred_element_type=F32)
            return 0

        lax.fori_loop(0, 2, go, 0)

        def regroup(i, _):
            at = pl.ds(pl.multiple_of(i * step * GROUP, step * GROUP), step * GROUP)
            to_messages(slot, time_buf[at, :half], time_buf[at, half:], pl.multiple_of(i * step * msg, step * msg))
            return 0

        lax.fori_loop(0, parts // step, regroup, 0)

    def to_chan(i, src, dst, peer, snd_sems, rcv_sems):
        return pltpu.make_async_remote_copy(
            src_ref=src, dst_ref=dst, send_sem=snd_sems.at[i], recv_sem=rcv_sems.at[i],
            device_id=(me, peer), device_id_type=MESH,
        )

    def cot_copy(i, owner, h, peer):
        ref = cots.at[owner, pl.ds(h * (blk // 2), blk // 2)]
        return to_chan(i, ref, ref, peer, cot_snd_sem, cot_rcv_sem)

    cot_y = [cot_copy(h, ch, h, y_peer) for h in range(2)]
    cot_core = to_chan(2, cots.at[ch], cots.at[ch], core_peer, cot_snd_sem, cot_rcv_sem)
    cot_far = [cot_copy(3 + h, y_peer, h, core_peer) for h in range(2)]

    loaded("fil")
    pack(K_SLOT, lambda r, c: fil_ref[r, c].astype(F32))
    loaded("cot")
    pl.semaphore_wait(barrier, parts + 1)
    cot_y[0].start()
    cot_y[1].start()
    cot_core.start()
    send(K_SLOT, False)
    loaded("ig", "val")

    def source(r, c):
        return ig_ref[r, c].astype(F32) * val_ref[r, c].astype(F32)

    pack(S_SLOT, source)
    send(S_SLOT, False)
    send(K_SLOT, True)
    loaded("w", "og")

    def d_block(b):
        at = pl.ds(pl.multiple_of(b * blk, blk), blk)
        d = lax.dot_general(cots[b], w_ref[...], (((1,), (1,)), ((), ())), preferred_element_type=F32)
        d_gated[at] = d
        time_buf[at] = d * og_ref[at].astype(F32)

    d_block(ch)
    cot_core.wait_recv()
    d_block(core_peer)
    for h in range(2):
        cot_y[h].wait_recv()
        cot_far[h].start()
    send(S_SLOT, True)
    d_block(y_peer)
    cot_far[0].wait_recv()
    cot_far[1].wait_recv()
    d_block(far_peer)
    pack(D_SLOT, lambda r, c: time_buf[r, c])
    send(D_SLOT, False)
    send(D_SLOT, True)

    loaded("across", "turn_re", "turn_im", "within_hi", "within_lo", "back")
    arrived(K_SLOT)
    forward(K_SLOT, 0)
    arrived(S_SLOT)
    forward(S_SLOT, 1)

    def conv_product(cols, cols_imag):
        a, b = spec[0, :, cols], spec[0, :, cols_imag]
        c, d = spec[1, :, cols], spec[1, :, cols_imag]
        return a * c - b * d, -(a * d + b * c)

    inverse(C_SLOT, conv_product)
    send(C_SLOT, False, back=True)
    send(C_SLOT, True, back=True)
    rcv[C_SLOT, message(my_slot)] = snd[C_SLOT, message(me)]
    arrived(D_SLOT)
    forward(D_SLOT, 2)

    def correlation(which):
        def product(cols, cols_imag):
            a, b = spec[which, :, cols], spec[which, :, cols_imag]
            c, d = spec[2, :, cols], spec[2, :, cols_imag]
            return a * c + b * d, b * c - a * d

        return product

    inverse(DS_SLOT, correlation(0))
    send(DS_SLOT, True, back=True, landing=ds_hbm)
    send(DS_SLOT, False, back=True, landing=ds_hbm)
    own_ds = pltpu.make_async_copy(snd.at[DS_SLOT, message(me)], ds_hbm.at[message(my_slot)], store_sem.at[0])
    own_ds.start()
    inverse(DK_SLOT, correlation(1))
    own_dk = pltpu.make_async_copy(snd.at[DK_SLOT, message(me)], dk_hbm.at[message(my_slot)], store_sem.at[1])
    own_dk.start()

    arrived(C_SLOT)

    def use_conv(h):
        at = pl.ds(pl.multiple_of(h * half, half), half)

        def go(t, _):
            cols = pl.ds(pl.multiple_of(t * tile, tile), tile)
            both = rcv[C_SLOT, pl.ds(pl.multiple_of(t * groups * msg, groups * msg), groups * msg)]
            both = both.astype(F32).reshape(groups, msg, half)
            conv = jnp.where(h == 0, both[:, :GROUP], both[:, GROUP:]).reshape(tile, half).T
            gated[at, cols] = (og_ref[at, cols].astype(F32) * conv).astype(BF16)
            d_og_buf[at, cols] = d_gated[at, cols] * conv
            return 0

        lax.fori_loop(0, tiles, go, 0)

    out_tile = min(512, dout)

    def project(j, of_core, store):
        at = pl.ds(pl.multiple_of((2 * j + of_core) * blk, blk), blk)

        def go(n, _):
            cols = pl.ds(pl.multiple_of(n * out_tile, out_tile), out_tile)
            store(cols, jnp.dot(gated[at], w_ref[:, cols], preferred_element_type=F32))
            return 0

        lax.fori_loop(0, dout // out_tile, go, 0)

    def store_peer(i):
        def store(cols, value):
            core_snd[i, :, cols] = value.astype(BF16)

        return store

    def store_mine(i):
        def store(cols, value):
            total_buf[i, :, cols] = value

        return store

    red_core = [to_chan(i, core_snd.at[i], core_rcv.at[i], core_peer, red_snd_sem, red_rcv_sem) for i in range(2)]
    red_y = to_chan(2, y_snd, y_rcv, y_peer, red_snd_sem, red_rcv_sem)
    use_conv(1 - high)
    project(1 - high, 1 - core, store_peer(0))
    red_core[0].start()
    project(1 - high, core, store_mine(0))
    red_core[0].wait_recv()
    y_snd[...] = (total_buf[0] + core_rcv[0].astype(F32)).astype(BF16)
    red_y.start()
    send(DK_SLOT, False, back=True, landing=dk_hbm)
    send(DK_SLOT, True, back=True, landing=dk_hbm)
    use_conv(high)
    d_og_out = pltpu.make_async_copy(d_og_buf, d_og_hbm, store_sem.at[2])
    d_og_out.start()
    project(high, 1 - core, store_peer(1))
    red_core[1].start()
    project(high, core, store_mine(1))
    red_core[1].wait_recv()
    total_buf[1] = total_buf[1] + core_rcv[1].astype(F32)
    red_y.wait_recv()
    out_buf[...] = (total_buf[1] + y_rcv[...].astype(F32)).astype(BF16)
    out_out = pltpu.make_async_copy(out_buf, out_hbm, store_sem.at[3])
    out_out.start()

    await_bytes(ds_hbm, rcv_sem.at[DS_SLOT])
    for slot in range(6):
        await_bytes(snd.at[slot], snd_sem.at[slot])
    for copy in (*cot_y, cot_core, *cot_far, *red_core, red_y):
        copy.wait_send()
    for copy in (own_ds, own_dk, d_og_out, out_out):
        copy.wait()
    await_bytes(dk_hbm, rcv_sem.at[DK_SLOT])


def finish(ig_ref, val_ref, ds_ref, dk_ref, d_og_in, out_in, d_ig_ref, d_val_ref, d_fil_ref, d_og_ref, out_ref):
    rows, tile = val_ref.shape
    half = rows // 2
    groups = tile // GROUP

    def positions(ref, h):
        both = ref[...].astype(F32).reshape(groups, 2 * GROUP, half)
        return both[:, h * GROUP : (h + 1) * GROUP].reshape(tile, half).T

    for h in range(2):
        at = pl.ds(h * half, half)
        grad = positions(ds_ref, h)
        d_ig_ref[at] = grad * val_ref[at].astype(F32)
        d_val_ref[at] = grad * ig_ref[at].astype(F32)
        d_fil_ref[at] = positions(dk_ref, h)
    d_og_ref[...] = d_og_in[...]
    out_ref[...] = out_in[...]


def on_device(out_gate, in_gate, values, filter_param, out_weight, out_cotangent):
    rows, width = values.shape
    parts = lax.axis_size("seq")
    blk, dout = out_cotangent.shape
    tables = make_tables(parts, rows)
    nk = tables[4].shape[0]
    msgs = (parts * 2 * GROUP, rows // 2)
    tile = min(TILE, width)
    tiles = width // tile
    operands = (out_gate, in_gate, values, filter_param, out_weight, out_cotangent, *tables)
    grad = jax.ShapeDtypeStruct((rows, width), F32)
    block_out = jax.ShapeDtypeStruct((blk, dout), BF16)
    raw = jax.ShapeDtypeStruct(msgs, BF16)
    anywhere = pl.BlockSpec(memory_space=pl.ANY)
    output, d_og, ds_raw, dk_raw = pl.pallas_call(
        kernel,
        out_shape=(block_out, grad, raw, raw),
        in_specs=[anywhere] * 12,
        out_specs=(anywhere,) * 4,
        scratch_shapes=[
            *(pltpu.VMEM(x.shape, x.dtype) for i, x in enumerate(operands) if i != 5),
            pltpu.VMEM((6, *msgs), BF16),
            pltpu.VMEM((4, *msgs), BF16),
            pltpu.VMEM((4, blk, dout), BF16),
            pltpu.VMEM((rows, width), F32),
            pltpu.VMEM((rows, width), F32),
            pltpu.VMEM((rows, width), BF16),
            pltpu.VMEM((rows, width), F32),
            pltpu.VMEM((parts * GROUP, rows), BF16),
            pltpu.VMEM((2 * nk, 2 * rows), BF16),
            pltpu.VMEM((4, nk, 2 * rows), F32),
            pltpu.VMEM((6 * nk, rows), BF16),
            pltpu.VMEM((2, blk, dout), BF16),
            pltpu.VMEM((2, blk, dout), BF16),
            pltpu.VMEM((blk, dout), BF16),
            pltpu.VMEM((blk, dout), BF16),
            pltpu.VMEM((2, blk, dout), F32),
            pltpu.VMEM((blk, dout), BF16),
            pltpu.SemaphoreType.DMA((12,)),
            pltpu.SemaphoreType.DMA((4,)),
            pltpu.SemaphoreType.DMA((6,)),
            pltpu.SemaphoreType.DMA((6,)),
            pltpu.SemaphoreType.DMA((5,)),
            pltpu.SemaphoreType.DMA((5,)),
            pltpu.SemaphoreType.DMA((3,)),
            pltpu.SemaphoreType.DMA((3,)),
        ],
        compiler_params=pltpu.CompilerParams(collective_id=0, has_side_effects=True, vmem_limit_bytes=60 * 2**20),
    )(*operands)
    by_channel = pl.BlockSpec((rows, tile), lambda t: (0, t))
    by_row = pl.BlockSpec((msgs[0] // tiles, msgs[1]), lambda t: (t, 0))
    out_rows = pl.BlockSpec((blk // tiles, dout), lambda t: (t, 0))
    d_ig, d_val, d_fil, d_og, output = pl.pallas_call(
        finish,
        grid=(tiles,),
        out_shape=(grad, grad, grad, grad, block_out),
        in_specs=[by_channel, by_channel, by_row, by_row, by_channel, out_rows],
        out_specs=(by_channel, by_channel, by_channel, by_channel, out_rows),
        compiler_params=pltpu.CompilerParams(vmem_limit_bytes=60 * 2**20),
    )(in_gate, values, ds_raw, dk_raw, d_og, output)
    return output, d_og, d_ig, d_val, d_fil


def solution(mesh):
    return jax.shard_map(
        on_device,
        mesh=mesh,
        in_specs=(
            P("seq", "chan"),
            P("seq", "chan"),
            P("seq", "chan"),
            P("seq", "chan"),
            P("chan", None),
            P(("seq", "chan"), None),
        ),
        out_specs=(
            P(("seq", "chan"), None),
            P("seq", "chan"),
            P("seq", "chan"),
            P("seq", "chan"),
            P("seq", "chan"),
        ),
        check_vma=False,
    )
```

```python
import functools
import math

import jax
import jax.numpy as jnp
import ml_dtypes
import numpy as np
from jax import lax
from jax.experimental import pallas as pl
from jax.experimental.pallas import tpu as pltpu
from jax.sharding import PartitionSpec as P

MESH = pl.DeviceIdType.MESH
F32 = jnp.float32
BF16 = jnp.bfloat16
GROUP = 8
TILE = 128
K_SLOT, S_SLOT, D_SLOT, C_SLOT, DS_SLOT, DK_SLOT = range(6)


def split_table(table):
    high = table.astype(np.float32).astype(ml_dtypes.bfloat16)
    low = (table - high.astype(np.float64)).astype(np.float32).astype(ml_dtypes.bfloat16)
    return high, low


def make_tables(parts, rows):
    total = parts * rows
    kept = parts // 2 + 1
    padded = kept + kept % 2
    k1 = np.arange(padded)
    shard = np.arange(parts)
    pos = np.arange(rows)
    eye = np.eye(GROUP)
    angle = 2.0 * np.pi * ((k1[:, None] * shard[None, :]) % parts) / parts
    across = np.concatenate([np.kron(np.cos(angle), eye), np.kron(-np.sin(angle), eye)], 0)
    across_table = np.concatenate(split_table(across), 0)
    weight = np.where((k1 == 0) | (k1 == parts // 2), 1.0, 2.0) * (k1 < kept)
    factor = weight / (total * math.sqrt(total))
    back = np.concatenate([np.kron((np.cos(angle) * factor[:, None]).T, eye), np.kron((np.sin(angle) * factor[:, None]).T, eye)], 1)
    back_high, back_low = split_table(back)
    back_table = np.concatenate([back_high, back_low, back_high], 1)
    square = 2.0 * np.pi * ((pos[:, None] * pos[None, :]) % rows) / rows
    within = np.block([[np.cos(square), -np.sin(square)], [np.sin(square), np.cos(square)]])
    within_table = split_table(within)[0]
    turn = 2.0 * np.pi * (k1[:, None] * pos[None, :]) / total
    turn_re = np.repeat(np.cos(turn), GROUP, 0).astype(np.float32)
    turn_im = np.repeat(-np.sin(turn), GROUP, 0).astype(np.float32)
    return across_table, within_table, back_table, turn_re, turn_im


def split_value(value):
    high = value.astype(BF16)
    return high, (value - high.astype(F32)).astype(BF16)


def by_fours(start, stop, do):
    for i in range(start, 4 if start else 0):
        do(i)

    def go(n, _):
        for i in range(4):
            do(n * 4 + i)
        return 0

    lax.fori_loop(1 if start else 0, stop // 4, go, 0)


def kernel(
    og_hbm, ig_hbm, val_hbm, fil_hbm, w_hbm, cot_hbm,
    across_hbm, within_hbm, back_hbm, turn_re_hbm, turn_im_hbm,
    out_hbm, d_og_hbm, ds_hbm, dk_hbm,
    og_ref, ig_ref, val_ref, fil_ref, w_ref,
    across_ref, within_ref, back_ref, turn_re_ref, turn_im_ref,
    snd, rcv, cots, d_gated, time_buf, gated, d_og_buf, chan_buf, lhs, spec, stack,
    core_snd, core_rcv, y_snd, y_rcv, total_buf, out_buf,
    load_sem, store_sem, snd_sem, rcv_sem, cot_snd_sem, cot_rcv_sem, red_snd_sem, red_rcv_sem,
):
    parts = lax.axis_size("seq")
    me, ch = lax.axis_index("seq"), lax.axis_index("chan")
    core, high = lax.rem(ch, 2), ch // 2
    core_peer = high * 2 + (1 - core)
    y_peer = (1 - high) * 2 + core
    far_peer = (1 - high) * 2 + (1 - core)
    rows, width = val_ref.shape
    half = rows // 2
    tile = min(TILE, width)
    tiles = width // tile
    groups = tile // GROUP
    msg = 2 * GROUP
    nk = turn_re_ref.shape[0]
    _, blk, dout = cots.shape
    my_tile, my_group = lax.rem(me, tiles), me // tiles
    my_slot = my_tile * groups + my_group

    loads = {}
    for i, (name, src, dst) in enumerate(
        (
            ("cot", cot_hbm, cots.at[ch]),
            ("fil", fil_hbm, fil_ref),
            ("ig", ig_hbm, ig_ref),
            ("val", val_hbm, val_ref),
            ("w", w_hbm, w_ref),
            ("og", og_hbm, og_ref),
            ("across", across_hbm, across_ref),
            ("turn_re", turn_re_hbm, turn_re_ref),
            ("turn_im", turn_im_hbm, turn_im_ref),
            ("within", within_hbm, within_ref),
            ("back", back_hbm, back_ref),
        )
    ):
        loads[name] = pltpu.make_async_copy(src, dst, load_sem.at[i])

    def loaded(*names):
        for name in names:
            loads[name].wait()

    loads["fil"].start()
    loads["cot"].start()

    barrier = pltpu.get_barrier_semaphore()

    def greet(d):
        pl.semaphore_signal(barrier, inc=1, device_id=(lax.rem(me + d, parts), ch), device_id_type=MESH)

    by_fours(1, parts, greet)
    pl.semaphore_signal(barrier, inc=1, device_id=(me, core_peer), device_id_type=MESH)
    pl.semaphore_signal(barrier, inc=1, device_id=(me, y_peer), device_id_type=MESH)

    for name, load in loads.items():
        if name not in ("fil", "cot"):
            load.start()

    def message(p):
        return pl.ds(pl.multiple_of(p * msg, msg), msg)

    near_parts = parts // 2
    side, place = me // near_parts, lax.rem(me, near_parts)

    def send(slot, crossing, back=False, landing=None):
        landing = rcv.at[slot] if landing is None else landing
        base = (1 - side if crossing else side) * near_parts

        def start(i):
            p = base + lax.rem(place + i * 13, near_parts)
            by_channel = lax.rem(p, tiles) * groups + p // tiles
            pltpu.make_async_remote_copy(
                src_ref=snd.at[slot, message(p if back else by_channel)],
                dst_ref=landing.at[message(my_slot if back else me)],
                send_sem=snd_sem.at[slot],
                recv_sem=rcv_sem.at[slot],
                device_id=(p, ch),
                device_id_type=MESH,
            ).start()

        by_fours(0 if crossing else 1, near_parts, start)

    def await_bytes(ref, sem):
        ref = ref.at[pl.ds(0, (parts - 1) * msg)]
        pltpu.make_async_copy(ref, ref, sem).wait()

    def arrived(slot):
        await_bytes(rcv.at[slot], rcv_sem.at[slot])

    def to_messages(slot, first, second, row):
        n = first.shape[0] // GROUP
        both = jnp.concatenate([first.reshape(n, GROUP, half), second.reshape(n, GROUP, half)], 1)
        snd[slot, pl.ds(row, n * msg)] = both.reshape(n * msg, half).astype(BF16)

    def pack(slot, load):
        def go(t, _):
            cols = pl.ds(pl.multiple_of(t * tile, tile), tile)
            first, second = (load(pl.ds(h * half, half), cols).T for h in range(2))
            to_messages(slot, first, second, pl.multiple_of(t * groups * msg, groups * msg))
            return 0

        lax.fori_loop(0, tiles, go, 0)
        rcv[slot, message(me)] = snd[slot, message(my_slot)]

    def turn(real, imag, cols):
        a, b = turn_re_ref[:, cols], turn_im_ref[:, cols]
        return real * a - imag * b, real * b + imag * a

    def put_lhs(real, imag, cols, cols_imag, fine):
        for value, at in ((real, cols), (imag, cols_imag)):
            if fine:
                hi, lo = split_value(value)
                lhs[:nk, at] = hi
                lhs[nk:, at] = lo
            else:
                lhs[:nk, at] = value.astype(BF16)

    def halves_of(h):
        return (
            pl.ds(pl.multiple_of(h * half, half), half),
            pl.ds(pl.multiple_of(rows + h * half, half), half),
        )

    def within(dst, fine):
        def go(j, _):
            cols = pl.ds(pl.multiple_of(j * half, half), half)
            if fine:
                both = jnp.dot(lhs[...], within_ref[:, cols], preferred_element_type=F32)
                spec[dst, :, cols] = both[:nk] + both[nk:]
            else:
                spec[dst, :, cols] = jnp.dot(lhs[:nk], within_ref[:, cols], preferred_element_type=F32)
            return 0

        lax.fori_loop(0, 4, go, 0)

    step = min(16, parts)

    def forward(slot, dst, fine):
        def regroup(i, _):
            both = rcv[slot, pl.ds(pl.multiple_of(i * step * msg, step * msg), step * msg)]
            both = both.astype(F32).reshape(step, msg, half)
            at = pl.ds(pl.multiple_of(i * step * GROUP, step * GROUP), step * GROUP)
            chan_buf[at, :half] = both[:, :GROUP].reshape(step * GROUP, half).astype(BF16)
            chan_buf[at, half:] = both[:, GROUP:].reshape(step * GROUP, half).astype(BF16)
            return 0

        lax.fori_loop(0, parts // step, regroup, 0)

        def go(h, _):
            cols, cols_imag = halves_of(h)
            if fine:
                y = jnp.dot(across_ref[...], chan_buf[:, cols], preferred_element_type=F32)
                y = y[: 2 * nk] + y[2 * nk :]
            else:
                y = jnp.dot(across_ref[: 2 * nk], chan_buf[:, cols], preferred_element_type=F32)
            real, imag = turn(y[:nk], y[nk:], cols)
            put_lhs(real, imag, cols, cols_imag, True)
            return 0

        lax.fori_loop(0, 2, go, 0)
        within(dst, True)

    def inverse(slot, product, fine):
        def fill(h, _):
            cols, cols_imag = halves_of(h)
            real, imag = product(cols, cols_imag)
            put_lhs(real, imag, cols, cols_imag, fine)
            return 0

        lax.fori_loop(0, 2, fill, 0)
        within(3, fine)

        def go(h, _):
            cols, cols_imag = halves_of(h)
            real, imag = turn(spec[3, :, cols], spec[3, :, cols_imag], cols)
            for i, value in enumerate((real, imag)):
                hi, lo = split_value(value)
                stack[i * nk : (i + 1) * nk, cols] = hi
                stack[(2 + i) * nk : (3 + i) * nk, cols] = hi
                if fine:
                    stack[(4 + i) * nk : (5 + i) * nk, cols] = lo
            if fine:
                time_buf[:, cols] = jnp.dot(back_ref[...], stack[:, cols], preferred_element_type=F32)
            else:
                time_buf[:, cols] = jnp.dot(
                    back_ref[:, : 4 * nk], stack[: 4 * nk, cols], preferred_element_type=F32
                )
            return 0

        lax.fori_loop(0, 2, go, 0)

        def regroup(i, _):
            at = pl.ds(pl.multiple_of(i * step * GROUP, step * GROUP), step * GROUP)
            to_messages(slot, time_buf[at, :half], time_buf[at, half:], pl.multiple_of(i * step * msg, step * msg))
            return 0

        lax.fori_loop(0, parts // step, regroup, 0)

    def to_chan(i, src, dst, peer, snd_sems, rcv_sems):
        return pltpu.make_async_remote_copy(
            src_ref=src, dst_ref=dst, send_sem=snd_sems.at[i], recv_sem=rcv_sems.at[i],
            device_id=(me, peer), device_id_type=MESH,
        )

    def cot_copy(i, owner, h, peer):
        ref = cots.at[owner, pl.ds(h * (blk // 2), blk // 2)]
        return to_chan(i, ref, ref, peer, cot_snd_sem, cot_rcv_sem)

    cot_y = [cot_copy(h, ch, h, y_peer) for h in range(2)]
    cot_core = to_chan(2, cots.at[ch], cots.at[ch], core_peer, cot_snd_sem, cot_rcv_sem)
    cot_far = [cot_copy(3 + h, y_peer, h, core_peer) for h in range(2)]

    loaded("fil")
    pack(K_SLOT, lambda r, c: fil_ref[r, c].astype(F32))
    loaded("cot")
    pl.semaphore_wait(barrier, parts + 1)
    cot_y[0].start()
    cot_y[1].start()
    cot_core.start()
    send(K_SLOT, False)
    loaded("ig", "val")

    def source(r, c):
        return ig_ref[r, c].astype(F32) * val_ref[r, c].astype(F32)

    pack(S_SLOT, source)
    send(S_SLOT, False)
    send(K_SLOT, True)
    loaded("w", "og")

    def d_block(b):
        at = pl.ds(pl.multiple_of(b * blk, blk), blk)
        d = lax.dot_general(cots[b], w_ref[...], (((1,), (1,)), ((), ())), preferred_element_type=F32)
        d_gated[at] = d
        time_buf[at] = d * og_ref[at].astype(F32)

    d_block(ch)
    cot_core.wait_recv()
    d_block(core_peer)
    for h in range(2):
        cot_y[h].wait_recv()
        cot_far[h].start()
    send(S_SLOT, True)
    d_block(y_peer)
    cot_far[0].wait_recv()
    cot_far[1].wait_recv()
    d_block(far_peer)
    pack(D_SLOT, lambda r, c: time_buf[r, c])
    send(D_SLOT, False)

    loaded("across", "turn_re", "turn_im", "within", "back")
    arrived(K_SLOT)
    forward(K_SLOT, 0, True)
    send(D_SLOT, True)
    arrived(S_SLOT)
    forward(S_SLOT, 1, True)

    def conv_product(cols, cols_imag):
        a, b = spec[0, :, cols], spec[0, :, cols_imag]
        c, d = spec[1, :, cols], spec[1, :, cols_imag]
        return a * c - b * d, -(a * d + b * c)

    inverse(C_SLOT, conv_product, True)
    send(C_SLOT, False, back=True)
    send(C_SLOT, True, back=True)
    rcv[C_SLOT, message(my_slot)] = snd[C_SLOT, message(me)]
    arrived(D_SLOT)
    forward(D_SLOT, 2, False)

    def correlation(which):
        def product(cols, cols_imag):
            a, b = spec[which, :, cols], spec[which, :, cols_imag]
            c, d = spec[2, :, cols], spec[2, :, cols_imag]
            return a * c + b * d, b * c - a * d

        return product

    inverse(DS_SLOT, correlation(0), False)
    send(DS_SLOT, True, back=True, landing=ds_hbm)
    send(DS_SLOT, False, back=True, landing=ds_hbm)
    own_ds = pltpu.make_async_copy(snd.at[DS_SLOT, message(me)], ds_hbm.at[message(my_slot)], store_sem.at[0])
    own_ds.start()

    arrived(C_SLOT)

    def use_conv(h):
        at = pl.ds(pl.multiple_of(h * half, half), half)

        def go(t, _):
            cols = pl.ds(pl.multiple_of(t * tile, tile), tile)
            both = rcv[C_SLOT, pl.ds(pl.multiple_of(t * groups * msg, groups * msg), groups * msg)]
            both = both.astype(F32).reshape(groups, msg, half)
            conv = jnp.where(h == 0, both[:, :GROUP], both[:, GROUP:]).reshape(tile, half).T
            gated[at, cols] = (og_ref[at, cols].astype(F32) * conv).astype(BF16)
            d_og_buf[at, cols] = d_gated[at, cols] * conv
            return 0

        lax.fori_loop(0, tiles, go, 0)

    out_tile = min(512, dout)

    def project(j, of_core, store):
        at = pl.ds(pl.multiple_of((2 * j + of_core) * blk, blk), blk)

        def go(n, _):
            cols = pl.ds(pl.multiple_of(n * out_tile, out_tile), out_tile)
            store(cols, jnp.dot(gated[at], w_ref[:, cols], preferred_element_type=F32))
            return 0

        lax.fori_loop(0, dout // out_tile, go, 0)

    def store_peer(i):
        def store(cols, value):
            core_snd[i, :, cols] = value.astype(BF16)

        return store

    def store_mine(i):
        def store(cols, value):
            total_buf[i, :, cols] = value

        return store

    red_core = [to_chan(i, core_snd.at[i], core_rcv.at[i], core_peer, red_snd_sem, red_rcv_sem) for i in range(2)]
    red_y = to_chan(2, y_snd, y_rcv, y_peer, red_snd_sem, red_rcv_sem)
    use_conv(1 - high)
    project(1 - high, 1 - core, store_peer(0))
    red_core[0].start()
    project(1 - high, core, store_mine(0))
    red_core[0].wait_recv()
    y_snd[...] = (total_buf[0] + core_rcv[0].astype(F32)).astype(BF16)
    red_y.start()
    inverse(DK_SLOT, correlation(1), False)
    own_dk = pltpu.make_async_copy(snd.at[DK_SLOT, message(me)], dk_hbm.at[message(my_slot)], store_sem.at[1])
    own_dk.start()
    send(DK_SLOT, False, back=True, landing=dk_hbm)
    send(DK_SLOT, True, back=True, landing=dk_hbm)
    use_conv(high)
    d_og_out = pltpu.make_async_copy(d_og_buf, d_og_hbm, store_sem.at[2])
    d_og_out.start()
    project(high, 1 - core, store_peer(1))
    red_core[1].start()
    project(high, core, store_mine(1))
    red_core[1].wait_recv()
    total_buf[1] = total_buf[1] + core_rcv[1].astype(F32)
    red_y.wait_recv()
    out_buf[...] = (total_buf[1] + y_rcv[...].astype(F32)).astype(BF16)
    out_out = pltpu.make_async_copy(out_buf, out_hbm, store_sem.at[3])
    out_out.start()

    await_bytes(ds_hbm, rcv_sem.at[DS_SLOT])
    for slot in range(6):
        await_bytes(snd.at[slot], snd_sem.at[slot])
    for copy in (*cot_y, cot_core, *cot_far, *red_core, red_y):
        copy.wait_send()
    for copy in (own_ds, own_dk, d_og_out, out_out):
        copy.wait()
    await_bytes(dk_hbm, rcv_sem.at[DK_SLOT])


def finish(ig_ref, val_ref, ds_ref, dk_ref, d_og_in, out_in, d_ig_ref, d_val_ref, d_fil_ref, d_og_ref, out_ref):
    rows, tile = val_ref.shape
    half = rows // 2
    groups = tile // GROUP

    def positions(ref, h):
        both = ref[...].astype(F32).reshape(groups, 2 * GROUP, half)
        return both[:, h * GROUP : (h + 1) * GROUP].reshape(tile, half).T

    for h in range(2):
        at = pl.ds(h * half, half)
        grad = positions(ds_ref, h)
        d_ig_ref[at] = grad * val_ref[at].astype(F32)
        d_val_ref[at] = grad * ig_ref[at].astype(F32)
        d_fil_ref[at] = positions(dk_ref, h)
    d_og_ref[...] = d_og_in[...]
    out_ref[...] = out_in[...]


def on_device(out_gate, in_gate, values, filter_param, out_weight, out_cotangent):
    rows, width = values.shape
    parts = lax.axis_size("seq")
    blk, dout = out_cotangent.shape
    tables = make_tables(parts, rows)
    nk = tables[3].shape[0]
    msgs = (parts * 2 * GROUP, rows // 2)
    tile = min(TILE, width)
    tiles = width // tile
    operands = (out_gate, in_gate, values, filter_param, out_weight, out_cotangent, *tables)
    grad = jax.ShapeDtypeStruct((rows, width), F32)
    block_out = jax.ShapeDtypeStruct((blk, dout), BF16)
    raw = jax.ShapeDtypeStruct(msgs, BF16)
    anywhere = pl.BlockSpec(memory_space=pl.ANY)
    output, d_og, ds_raw, dk_raw = pl.pallas_call(
        kernel,
        out_shape=(block_out, grad, raw, raw),
        in_specs=[anywhere] * 11,
        out_specs=(anywhere,) * 4,
        scratch_shapes=[
            *(pltpu.VMEM(x.shape, x.dtype) for i, x in enumerate(operands) if i != 5),
            pltpu.VMEM((6, *msgs), BF16),
            pltpu.VMEM((4, *msgs), BF16),
            pltpu.VMEM((4, blk, dout), BF16),
            pltpu.VMEM((rows, width), F32),
            pltpu.VMEM((rows, width), F32),
            pltpu.VMEM((rows, width), BF16),
            pltpu.VMEM((rows, width), F32),
            pltpu.VMEM((parts * GROUP, rows), BF16),
            pltpu.VMEM((2 * nk, 2 * rows), BF16),
            pltpu.VMEM((4, nk, 2 * rows), F32),
            pltpu.VMEM((6 * nk, rows), BF16),
            pltpu.VMEM((2, blk, dout), BF16),
            pltpu.VMEM((2, blk, dout), BF16),
            pltpu.VMEM((blk, dout), BF16),
            pltpu.VMEM((blk, dout), BF16),
            pltpu.VMEM((2, blk, dout), F32),
            pltpu.VMEM((blk, dout), BF16),
            pltpu.SemaphoreType.DMA((11,)),
            pltpu.SemaphoreType.DMA((4,)),
            pltpu.SemaphoreType.DMA((6,)),
            pltpu.SemaphoreType.DMA((6,)),
            pltpu.SemaphoreType.DMA((5,)),
            pltpu.SemaphoreType.DMA((5,)),
            pltpu.SemaphoreType.DMA((3,)),
            pltpu.SemaphoreType.DMA((3,)),
        ],
        compiler_params=pltpu.CompilerParams(collective_id=0, has_side_effects=True, vmem_limit_bytes=60 * 2**20),
    )(*operands)
    by_channel = pl.BlockSpec((rows, tile), lambda t: (0, t))
    by_row = pl.BlockSpec((msgs[0] // tiles, msgs[1]), lambda t: (t, 0))
    out_rows = pl.BlockSpec((blk // tiles, dout), lambda t: (t, 0))
    d_ig, d_val, d_fil, d_og, output = pl.pallas_call(
        finish,
        grid=(tiles,),
        out_shape=(grad, grad, grad, grad, block_out),
        in_specs=[by_channel, by_channel, by_row, by_row, by_channel, out_rows],
        out_specs=(by_channel, by_channel, by_channel, by_channel, out_rows),
        compiler_params=pltpu.CompilerParams(vmem_limit_bytes=60 * 2**20),
    )(in_gate, values, ds_raw, dk_raw, d_og, output)
    return output, d_og, d_ig, d_val, d_fil


def solution(mesh):
    return jax.shard_map(
        on_device,
        mesh=mesh,
        in_specs=(
            P("seq", "chan"),
            P("seq", "chan"),
            P("seq", "chan"),
            P("seq", "chan"),
            P("chan", None),
            P(("seq", "chan"), None),
        ),
        out_specs=(
            P(("seq", "chan"), None),
            P("seq", "chan"),
            P("seq", "chan"),
            P("seq", "chan"),
            P("seq", "chan"),
        ),
        check_vma=False,
    )
```

```python
import functools
import math

import jax
import jax.numpy as jnp
import ml_dtypes
import numpy as np
from jax import lax
from jax.experimental import pallas as pl
from jax.experimental.pallas import tpu as pltpu
from jax.sharding import PartitionSpec as P

MESH = pl.DeviceIdType.MESH
F32 = jnp.float32
BF16 = jnp.bfloat16
GROUP = 8
TILE = 128
K_SLOT, S_SLOT, D_SLOT, C_SLOT, DS_SLOT, DK_SLOT = range(6)


def split_table(table):
    high = table.astype(np.float32).astype(ml_dtypes.bfloat16)
    low = (table - high.astype(np.float64)).astype(np.float32).astype(ml_dtypes.bfloat16)
    return high, low


def make_tables(parts, rows):
    total = parts * rows
    kept = parts // 2 + 1
    padded = kept + kept % 2
    k1 = np.arange(padded)
    shard = np.arange(parts)
    pos = np.arange(rows)
    eye = np.eye(GROUP)
    angle = 2.0 * np.pi * ((k1[:, None] * shard[None, :]) % parts) / parts
    across = np.concatenate([np.kron(np.cos(angle), eye), np.kron(-np.sin(angle), eye)], 0)
    across_table = np.concatenate(split_table(across), 0)
    weight = np.where((k1 == 0) | (k1 == parts // 2), 1.0, 2.0) * (k1 < kept)
    factor = weight / (total * math.sqrt(total))
    back = np.concatenate([np.kron((np.cos(angle) * factor[:, None]).T, eye), np.kron((np.sin(angle) * factor[:, None]).T, eye)], 1)
    back_high, back_low = split_table(back)
    back_table = np.concatenate([back_high, back_low, back_high], 1)
    square = 2.0 * np.pi * ((pos[:, None] * pos[None, :]) % rows) / rows
    within = np.block([[np.cos(square), -np.sin(square)], [np.sin(square), np.cos(square)]])
    within_table = split_table(within)[0]
    turn = 2.0 * np.pi * (k1[:, None] * pos[None, :]) / total
    turn_re = np.repeat(np.cos(turn), GROUP, 0).astype(np.float32)
    turn_im = np.repeat(-np.sin(turn), GROUP, 0).astype(np.float32)
    return across_table, within_table, back_table, turn_re, turn_im


def split_value(value):
    high = value.astype(BF16)
    return high, (value - high.astype(F32)).astype(BF16)


def by_fours(start, stop, do):
    for i in range(start, 4 if start else 0):
        do(i)

    def go(n, _):
        for i in range(4):
            do(n * 4 + i)
        return 0

    lax.fori_loop(1 if start else 0, stop // 4, go, 0)


def kernel(
    og_hbm, ig_hbm, val_hbm, fil_hbm, w_hbm, cot_hbm,
    across_hbm, within_hbm, back_hbm, turn_re_hbm, turn_im_hbm,
    out_hbm, d_og_hbm, ds_hbm, dk_hbm,
    og_ref, ig_ref, val_ref, fil_ref, w_ref,
    across_ref, within_ref, back_ref, turn_re_ref, turn_im_ref,
    snd, rcv, cots, d_gated, time_buf, gated, d_og_buf, ds_buf, chan_buf, lhs, spec, stack,
    core_snd, core_rcv, y_snd, y_rcv, total_buf, out_buf,
    load_sem, store_sem, snd_sem, rcv_sem, cot_snd_sem, cot_rcv_sem, red_snd_sem, red_rcv_sem,
):
    parts = lax.axis_size("seq")
    me, ch = lax.axis_index("seq"), lax.axis_index("chan")
    core, high = lax.rem(ch, 2), ch // 2
    core_peer = high * 2 + (1 - core)
    y_peer = (1 - high) * 2 + core
    far_peer = (1 - high) * 2 + (1 - core)
    rows, width = val_ref.shape
    half = rows // 2
    tile = min(TILE, width)
    tiles = width // tile
    groups = tile // GROUP
    msg = 2 * GROUP
    nk = turn_re_ref.shape[0]
    _, blk, dout = cots.shape
    my_tile, my_group = lax.rem(me, tiles), me // tiles
    my_slot = my_tile * groups + my_group

    loads = {}
    for i, (name, src, dst) in enumerate(
        (
            ("cot", cot_hbm, cots.at[ch]),
            ("fil", fil_hbm, fil_ref),
            ("ig", ig_hbm, ig_ref),
            ("val", val_hbm, val_ref),
            ("w", w_hbm, w_ref),
            ("og", og_hbm, og_ref),
            ("across", across_hbm, across_ref),
            ("turn_re", turn_re_hbm, turn_re_ref),
            ("turn_im", turn_im_hbm, turn_im_ref),
            ("within", within_hbm, within_ref),
            ("back", back_hbm, back_ref),
        )
    ):
        loads[name] = pltpu.make_async_copy(src, dst, load_sem.at[i])

    def loaded(*names):
        for name in names:
            loads[name].wait()

    loads["fil"].start()
    loads["cot"].start()

    barrier = pltpu.get_barrier_semaphore()

    def greet(d):
        pl.semaphore_signal(barrier, inc=1, device_id=(lax.rem(me + d, parts), ch), device_id_type=MESH)

    by_fours(1, parts, greet)
    pl.semaphore_signal(barrier, inc=1, device_id=(me, core_peer), device_id_type=MESH)
    pl.semaphore_signal(barrier, inc=1, device_id=(me, y_peer), device_id_type=MESH)

    for name, load in loads.items():
        if name not in ("fil", "cot"):
            load.start()

    def message(p):
        return pl.ds(pl.multiple_of(p * msg, msg), msg)

    near_parts = parts // 2
    side, place = me // near_parts, lax.rem(me, near_parts)

    def send(slot, crossing, back=False, landing=None):
        landing = rcv.at[slot] if landing is None else landing
        base = (1 - side if crossing else side) * near_parts

        def start(i):
            p = base + lax.rem(place + i * 13, near_parts)
            by_channel = lax.rem(p, tiles) * groups + p // tiles
            pltpu.make_async_remote_copy(
                src_ref=snd.at[slot, message(p if back else by_channel)],
                dst_ref=landing.at[message(my_slot if back else me)],
                send_sem=snd_sem.at[slot],
                recv_sem=rcv_sem.at[slot],
                device_id=(p, ch),
                device_id_type=MESH,
            ).start()

        by_fours(0 if crossing else 1, near_parts, start)

    def await_bytes(ref, sem):
        ref = ref.at[pl.ds(0, (parts - 1) * msg)]
        pltpu.make_async_copy(ref, ref, sem).wait()

    def arrived(slot):
        await_bytes(rcv.at[slot], rcv_sem.at[slot])

    def to_messages(slot, first, second, row):
        n = first.shape[0] // GROUP
        both = jnp.concatenate([first.reshape(n, GROUP, half), second.reshape(n, GROUP, half)], 1)
        snd[slot, pl.ds(row, n * msg)] = both.reshape(n * msg, half).astype(BF16)

    def pack(slot, load):
        def go(t, _):
            cols = pl.ds(pl.multiple_of(t * tile, tile), tile)
            first, second = (load(pl.ds(h * half, half), cols).T for h in range(2))
            to_messages(slot, first, second, pl.multiple_of(t * groups * msg, groups * msg))
            return 0

        lax.fori_loop(0, tiles, go, 0)
        rcv[slot, message(me)] = snd[slot, message(my_slot)]

    def turn(real, imag, cols):
        a, b = turn_re_ref[:, cols], turn_im_ref[:, cols]
        return real * a - imag * b, real * b + imag * a

    def put_lhs(real, imag, cols, cols_imag, fine):
        for value, at in ((real, cols), (imag, cols_imag)):
            if fine:
                hi, lo = split_value(value)
                lhs[:nk, at] = hi
                lhs[nk:, at] = lo
            else:
                lhs[:nk, at] = value.astype(BF16)

    def halves_of(h):
        return (
            pl.ds(pl.multiple_of(h * half, half), half),
            pl.ds(pl.multiple_of(rows + h * half, half), half),
        )

    def within(dst, fine):
        def go(j, _):
            cols = pl.ds(pl.multiple_of(j * half, half), half)
            if fine:
                both = jnp.dot(lhs[...], within_ref[:, cols], preferred_element_type=F32)
                spec[dst, :, cols] = both[:nk] + both[nk:]
            else:
                spec[dst, :, cols] = jnp.dot(lhs[:nk], within_ref[:, cols], preferred_element_type=F32)
            return 0

        lax.fori_loop(0, 4, go, 0)

    step = min(16, parts)

    def forward(slot, dst, fine):
        def regroup(i, _):
            both = rcv[slot, pl.ds(pl.multiple_of(i * step * msg, step * msg), step * msg)]
            both = both.astype(F32).reshape(step, msg, half)
            at = pl.ds(pl.multiple_of(i * step * GROUP, step * GROUP), step * GROUP)
            chan_buf[at, :half] = both[:, :GROUP].reshape(step * GROUP, half).astype(BF16)
            chan_buf[at, half:] = both[:, GROUP:].reshape(step * GROUP, half).astype(BF16)
            return 0

        lax.fori_loop(0, parts // step, regroup, 0)

        def go(h, _):
            cols, cols_imag = halves_of(h)
            if fine:
                y = jnp.dot(across_ref[...], chan_buf[:, cols], preferred_element_type=F32)
                y = y[: 2 * nk] + y[2 * nk :]
            else:
                y = jnp.dot(across_ref[: 2 * nk], chan_buf[:, cols], preferred_element_type=F32)
            real, imag = turn(y[:nk], y[nk:], cols)
            put_lhs(real, imag, cols, cols_imag, True)
            return 0

        lax.fori_loop(0, 2, go, 0)
        within(dst, True)

    def inverse(slot, product, fine):
        def fill(h, _):
            cols, cols_imag = halves_of(h)
            real, imag = product(cols, cols_imag)
            put_lhs(real, imag, cols, cols_imag, fine)
            return 0

        lax.fori_loop(0, 2, fill, 0)
        within(3, fine)

        def go(h, _):
            cols, cols_imag = halves_of(h)
            real, imag = turn(spec[3, :, cols], spec[3, :, cols_imag], cols)
            for i, value in enumerate((real, imag)):
                hi, lo = split_value(value)
                stack[i * nk : (i + 1) * nk, cols] = hi
                stack[(2 + i) * nk : (3 + i) * nk, cols] = hi
                if fine:
                    stack[(4 + i) * nk : (5 + i) * nk, cols] = lo
            if fine:
                time_buf[:, cols] = jnp.dot(back_ref[...], stack[:, cols], preferred_element_type=F32)
            else:
                time_buf[:, cols] = jnp.dot(
                    back_ref[:, : 4 * nk], stack[: 4 * nk, cols], preferred_element_type=F32
                )
            return 0

        lax.fori_loop(0, 2, go, 0)

        def regroup(i, _):
            at = pl.ds(pl.multiple_of(i * step * GROUP, step * GROUP), step * GROUP)
            to_messages(slot, time_buf[at, :half], time_buf[at, half:], pl.multiple_of(i * step * msg, step * msg))
            return 0

        lax.fori_loop(0, parts // step, regroup, 0)

    def to_chan(i, src, dst, peer, snd_sems, rcv_sems):
        return pltpu.make_async_remote_copy(
            src_ref=src, dst_ref=dst, send_sem=snd_sems.at[i], recv_sem=rcv_sems.at[i],
            device_id=(me, peer), device_id_type=MESH,
        )

    def cot_copy(i, owner, h, peer):
        ref = cots.at[owner, pl.ds(h * (blk // 2), blk // 2)]
        return to_chan(i, ref, ref, peer, cot_snd_sem, cot_rcv_sem)

    cot_y = [cot_copy(h, ch, h, y_peer) for h in range(2)]
    cot_core = to_chan(2, cots.at[ch], cots.at[ch], core_peer, cot_snd_sem, cot_rcv_sem)
    cot_far = [cot_copy(3 + h, y_peer, h, core_peer) for h in range(2)]

    loaded("fil")
    pack(K_SLOT, lambda r, c: fil_ref[r, c].astype(F32))
    loaded("cot")
    pl.semaphore_wait(barrier, parts + 1)
    cot_y[0].start()
    cot_y[1].start()
    cot_core.start()
    send(K_SLOT, False)
    loaded("ig", "val")

    def source(r, c):
        return ig_ref[r, c].astype(F32) * val_ref[r, c].astype(F32)

    pack(S_SLOT, source)
    send(S_SLOT, False)
    send(K_SLOT, True)
    loaded("w", "og")

    def d_block(b):
        at = pl.ds(pl.multiple_of(b * blk, blk), blk)
        d = lax.dot_general(cots[b], w_ref[...], (((1,), (1,)), ((), ())), preferred_element_type=F32)
        d_gated[at] = d
        time_buf[at] = d * og_ref[at].astype(F32)

    d_block(ch)
    cot_core.wait_recv()
    d_block(core_peer)
    for h in range(2):
        cot_y[h].wait_recv()
        cot_far[h].start()
    send(S_SLOT, True)
    d_block(y_peer)
    cot_far[0].wait_recv()
    cot_far[1].wait_recv()
    d_block(far_peer)
    pack(D_SLOT, lambda r, c: time_buf[r, c])
    send(D_SLOT, False)

    loaded("across", "turn_re", "turn_im", "within", "back")
    arrived(K_SLOT)
    forward(K_SLOT, 0, True)
    send(D_SLOT, True)
    arrived(S_SLOT)
    forward(S_SLOT, 1, True)

    def conv_product(cols, cols_imag):
        a, b = spec[0, :, cols], spec[0, :, cols_imag]
        c, d = spec[1, :, cols], spec[1, :, cols_imag]
        return a * c - b * d, -(a * d + b * c)

    inverse(C_SLOT, conv_product, True)
    send(C_SLOT, False, back=True)
    send(C_SLOT, True, back=True)
    rcv[C_SLOT, message(my_slot)] = snd[C_SLOT, message(me)]
    arrived(D_SLOT)
    forward(D_SLOT, 2, False)

    def correlation(which):
        def product(cols, cols_imag):
            a, b = spec[which, :, cols], spec[which, :, cols_imag]
            c, d = spec[2, :, cols], spec[2, :, cols_imag]
            return a * c + b * d, b * c - a * d

        return product

    inverse(DS_SLOT, correlation(0), False)
    send(DS_SLOT, True, back=True)
    send(DS_SLOT, False, back=True)
    rcv[DS_SLOT, message(my_slot)] = snd[DS_SLOT, message(me)]

    arrived(C_SLOT)

    def unpack_half(slot, h, store):
        at = pl.ds(pl.multiple_of(h * half, half), half)

        def go(t, _):
            cols = pl.ds(pl.multiple_of(t * tile, tile), tile)
            both = rcv[slot, pl.ds(pl.multiple_of(t * groups * msg, groups * msg), groups * msg)]
            both = both.astype(F32).reshape(groups, msg, half)
            store(at, cols, jnp.where(h == 0, both[:, :GROUP], both[:, GROUP:]).reshape(tile, half).T)
            return 0

        lax.fori_loop(0, tiles, go, 0)

    def use_conv(h):
        def store(at, cols, conv):
            gated[at, cols] = (og_ref[at, cols].astype(F32) * conv).astype(BF16)
            d_og_buf[at, cols] = (d_gated[at, cols] * conv).astype(BF16)

        unpack_half(C_SLOT, h, store)

    out_tile = min(512, dout)

    def project(j, of_core, store):
        at = pl.ds(pl.multiple_of((2 * j + of_core) * blk, blk), blk)

        def go(n, _):
            cols = pl.ds(pl.multiple_of(n * out_tile, out_tile), out_tile)
            store(cols, jnp.dot(gated[at], w_ref[:, cols], preferred_element_type=F32))
            return 0

        lax.fori_loop(0, dout // out_tile, go, 0)

    def store_peer(i):
        def store(cols, value):
            core_snd[i, :, cols] = value.astype(BF16)

        return store

    def store_mine(i):
        def store(cols, value):
            total_buf[i, :, cols] = value

        return store

    red_core = [to_chan(i, core_snd.at[i], core_rcv.at[i], core_peer, red_snd_sem, red_rcv_sem) for i in range(2)]
    red_y = to_chan(2, y_snd, y_rcv, y_peer, red_snd_sem, red_rcv_sem)
    use_conv(1 - high)
    project(1 - high, 1 - core, store_peer(0))
    red_core[0].start()
    project(1 - high, core, store_mine(0))
    red_core[0].wait_recv()
    y_snd[...] = (total_buf[0] + core_rcv[0].astype(F32)).astype(BF16)
    red_y.start()
    inverse(DK_SLOT, correlation(1), False)
    own_dk = pltpu.make_async_copy(snd.at[DK_SLOT, message(me)], dk_hbm.at[message(my_slot)], store_sem.at[1])
    own_dk.start()
    send(DK_SLOT, False, back=True, landing=dk_hbm)
    send(DK_SLOT, True, back=True, landing=dk_hbm)
    use_conv(high)
    d_og_out = pltpu.make_async_copy(d_og_buf, d_og_hbm, store_sem.at[2])
    d_og_out.start()
    project(high, 1 - core, store_peer(1))
    red_core[1].start()
    project(high, core, store_mine(1))
    red_core[1].wait_recv()
    total_buf[1] = total_buf[1] + core_rcv[1].astype(F32)
    red_y.wait_recv()
    out_buf[...] = (total_buf[1] + y_rcv[...].astype(F32)).astype(BF16)
    out_out = pltpu.make_async_copy(out_buf, out_hbm, store_sem.at[3])
    out_out.start()

    def use_source(at, cols, grad):
        ds_buf[at, cols] = grad.astype(BF16)

    arrived(DS_SLOT)
    for h in range(2):
        unpack_half(DS_SLOT, h, use_source)
    ds_out = pltpu.make_async_copy(ds_buf, ds_hbm, store_sem.at[0])
    ds_out.start()
    for slot in range(6):
        await_bytes(snd.at[slot], snd_sem.at[slot])
    for copy in (*cot_y, cot_core, *cot_far, *red_core, red_y):
        copy.wait_send()
    for copy in (ds_out, own_dk, d_og_out, out_out):
        copy.wait()
    await_bytes(dk_hbm, rcv_sem.at[DK_SLOT])


def finish(
    ig_hbm, val_hbm, ds_hbm, dk_hbm, d_og_in_hbm, out_in_hbm,
    d_ig_hbm, d_val_hbm, d_fil_hbm, d_og_hbm, out_hbm,
    ig, val, ds, dk, d_og_in, d_ig, d_val, d_fil, d_og, load_sem, store_sem,
):
    rows, width = ig.shape
    half = rows // 2
    loads, stores = [], []

    def load(src, dst):
        loads.append(pltpu.make_async_copy(src, dst, load_sem.at[len(loads)]))
        loads[-1].start()

    def store(src, dst):
        stores.append(pltpu.make_async_copy(src, dst, store_sem.at[len(stores)]))
        stores[-1].start()

    halves = [pl.ds(h * half, half) for h in range(2)]
    for at in halves:
        for src, dst in ((ds_hbm, ds), (val_hbm, val), (ig_hbm, ig)):
            load(src.at[at], dst.at[at])
    load(dk_hbm, dk)
    load(d_og_in_hbm, d_og_in)
    store(out_in_hbm, out_hbm)
    for h, at in enumerate(halves):
        for copy in loads[3 * h : 3 * h + 3]:
            copy.wait()
        grad = ds[at].astype(F32)
        d_ig[at] = grad * val[at].astype(F32)
        store(d_ig.at[at], d_ig_hbm.at[at])
        d_val[at] = grad * ig[at].astype(F32)
        store(d_val.at[at], d_val_hbm.at[at])
    tile = min(TILE, width)
    msgs = 2 * tile
    loads[6].wait()
    for h, at in enumerate(halves):
        for t in range(width // tile):
            both = dk[pl.ds(t * msgs, msgs)].astype(F32).reshape(tile // GROUP, 2 * GROUP, half)
            d_fil[at, pl.ds(t * tile, tile)] = both[:, h * GROUP : (h + 1) * GROUP].reshape(tile, half).T
        store(d_fil.at[at], d_fil_hbm.at[at])
    loads[7].wait()
    d_og[...] = d_og_in[...].astype(F32)
    store(d_og, d_og_hbm)
    for copy in stores:
        copy.wait()


def on_device(out_gate, in_gate, values, filter_param, out_weight, out_cotangent):
    rows, width = values.shape
    parts = lax.axis_size("seq")
    blk, dout = out_cotangent.shape
    tables = make_tables(parts, rows)
    nk = tables[3].shape[0]
    msgs = (parts * 2 * GROUP, rows // 2)
    operands = (out_gate, in_gate, values, filter_param, out_weight, out_cotangent, *tables)
    grad = jax.ShapeDtypeStruct((rows, width), F32)
    block_out = jax.ShapeDtypeStruct((blk, dout), BF16)
    raw = jax.ShapeDtypeStruct(msgs, BF16)
    short = jax.ShapeDtypeStruct((rows, width), BF16)
    anywhere = pl.BlockSpec(memory_space=pl.ANY)
    output, d_og, ds_raw, dk_raw = pl.pallas_call(
        kernel,
        out_shape=(block_out, short, short, raw),
        in_specs=[anywhere] * 11,
        out_specs=(anywhere,) * 4,
        scratch_shapes=[
            *(pltpu.VMEM(x.shape, x.dtype) for i, x in enumerate(operands) if i != 5),
            pltpu.VMEM((6, *msgs), BF16),
            pltpu.VMEM((5, *msgs), BF16),
            pltpu.VMEM((4, blk, dout), BF16),
            pltpu.VMEM((rows, width), F32),
            pltpu.VMEM((rows, width), F32),
            pltpu.VMEM((rows, width), BF16),
            pltpu.VMEM((rows, width), BF16),
            pltpu.VMEM((rows, width), BF16),
            pltpu.VMEM((parts * GROUP, rows), BF16),
            pltpu.VMEM((2 * nk, 2 * rows), BF16),
            pltpu.VMEM((4, nk, 2 * rows), F32),
            pltpu.VMEM((6 * nk, rows), BF16),
            pltpu.VMEM((2, blk, dout), BF16),
            pltpu.VMEM((2, blk, dout), BF16),
            pltpu.VMEM((blk, dout), BF16),
            pltpu.VMEM((blk, dout), BF16),
            pltpu.VMEM((2, blk, dout), F32),
            pltpu.VMEM((blk, dout), BF16),
            pltpu.SemaphoreType.DMA((11,)),
            pltpu.SemaphoreType.DMA((4,)),
            pltpu.SemaphoreType.DMA((6,)),
            pltpu.SemaphoreType.DMA((6,)),
            pltpu.SemaphoreType.DMA((5,)),
            pltpu.SemaphoreType.DMA((5,)),
            pltpu.SemaphoreType.DMA((3,)),
            pltpu.SemaphoreType.DMA((3,)),
        ],
        compiler_params=pltpu.CompilerParams(collective_id=0, has_side_effects=True, vmem_limit_bytes=60 * 2**20),
    )(*operands)
    d_ig, d_val, d_fil, d_og, output = pl.pallas_call(
        finish,
        out_shape=(grad, grad, grad, grad, block_out),
        in_specs=[anywhere] * 6,
        out_specs=(anywhere,) * 5,
        scratch_shapes=[
            *([pltpu.VMEM((rows, width), BF16)] * 3),
            pltpu.VMEM(msgs, BF16),
            pltpu.VMEM((rows, width), BF16),
            *([pltpu.VMEM((rows, width), F32)] * 4),
            pltpu.SemaphoreType.DMA((8,)),
            pltpu.SemaphoreType.DMA((8,)),
        ],
        compiler_params=pltpu.CompilerParams(vmem_limit_bytes=60 * 2**20),
    )(in_gate, values, ds_raw, dk_raw, d_og, output)
    return output, d_og, d_ig, d_val, d_fil


def solution(mesh):
    return jax.shard_map(
        on_device,
        mesh=mesh,
        in_specs=(
            P("seq", "chan"),
            P("seq", "chan"),
            P("seq", "chan"),
            P("seq", "chan"),
            P("chan", None),
            P(("seq", "chan"), None),
        ),
        out_specs=(
            P(("seq", "chan"), None),
            P("seq", "chan"),
            P("seq", "chan"),
            P("seq", "chan"),
            P("seq", "chan"),
        ),
        check_vma=False,
    )
```

```python
import functools
import math

import jax
import jax.numpy as jnp
import ml_dtypes
import numpy as np
from jax import lax
from jax.experimental import pallas as pl
from jax.experimental.pallas import tpu as pltpu
from jax.sharding import PartitionSpec as P

MESH = pl.DeviceIdType.MESH
F32 = jnp.float32
BF16 = jnp.bfloat16
GROUP = 8
TILE = 128
K_SLOT, S_SLOT, D_SLOT, C_SLOT, DS_SLOT, DK_SLOT = range(6)


def split_table(table):
    high = table.astype(np.float32).astype(ml_dtypes.bfloat16)
    low = (table - high.astype(np.float64)).astype(np.float32).astype(ml_dtypes.bfloat16)
    return high, low


def make_tables(parts, rows):
    total = parts * rows
    kept = parts // 2 + 1
    padded = kept + kept % 2
    k1 = np.arange(padded)
    shard = np.arange(parts)
    pos = np.arange(rows)
    eye = np.eye(GROUP)
    angle = 2.0 * np.pi * ((k1[:, None] * shard[None, :]) % parts) / parts
    across = np.concatenate([np.kron(np.cos(angle), eye), np.kron(-np.sin(angle), eye)], 0)
    across_table = np.concatenate(split_table(across), 0)
    weight = np.where((k1 == 0) | (k1 == parts // 2), 1.0, 2.0) * (k1 < kept)
    factor = weight / (total * math.sqrt(total))
    back = np.concatenate([np.kron((np.cos(angle) * factor[:, None]).T, eye), np.kron((np.sin(angle) * factor[:, None]).T, eye)], 1)
    back_high, back_low = split_table(back)
    back_table = np.concatenate([back_high, back_low, back_high], 1)
    square = 2.0 * np.pi * ((pos[:, None] * pos[None, :]) % rows) / rows
    within = np.block([[np.cos(square), -np.sin(square)], [np.sin(square), np.cos(square)]])
    within_table = split_table(within)[0]
    turn = 2.0 * np.pi * (k1[:, None] * pos[None, :]) / total
    turn_re = np.repeat(np.cos(turn), GROUP, 0).astype(np.float32)
    turn_im = np.repeat(-np.sin(turn), GROUP, 0).astype(np.float32)
    return across_table, within_table, back_table, turn_re, turn_im


def split_value(value):
    high = value.astype(BF16)
    return high, (value - high.astype(F32)).astype(BF16)


def by_fours(start, stop, do):
    for i in range(start, 4 if start else 0):
        do(i)

    def go(n, _):
        for i in range(4):
            do(n * 4 + i)
        return 0

    lax.fori_loop(1 if start else 0, stop // 4, go, 0)


def kernel(
    og_hbm, ig_hbm, val_hbm, fil_hbm, w_hbm, cot_hbm,
    across_hbm, within_hbm, back_hbm, turn_re_hbm, turn_im_hbm,
    out_hbm, d_og_hbm, ds_hbm, dk_hbm,
    og_ref, ig_ref, val_ref, fil_ref, w_ref,
    across_ref, within_ref, back_ref, turn_re_ref, turn_im_ref,
    snd, rcv, cots, d_gated, time_buf, gated, d_og_buf, ds_buf, chan_buf, lhs, spec, stack,
    core_snd, core_rcv, y_snd, y_rcv, total_buf, out_buf,
    load_sem, store_sem, snd_sem, rcv_sem, cot_snd_sem, cot_rcv_sem, red_snd_sem, red_rcv_sem,
):
    parts = lax.axis_size("seq")
    me, ch = lax.axis_index("seq"), lax.axis_index("chan")
    core, high = lax.rem(ch, 2), ch // 2
    core_peer = high * 2 + (1 - core)
    y_peer = (1 - high) * 2 + core
    far_peer = (1 - high) * 2 + (1 - core)
    rows, width = val_ref.shape
    half = rows // 2
    tile = min(TILE, width)
    tiles = width // tile
    groups = tile // GROUP
    msg = 2 * GROUP
    nk = turn_re_ref.shape[0]
    _, blk, dout = cots.shape
    my_tile, my_group = lax.rem(me, tiles), me // tiles
    my_slot = my_tile * groups + my_group

    loads = {}
    for i, (name, src, dst) in enumerate(
        (
            ("cot", cot_hbm, cots.at[ch]),
            ("fil", fil_hbm, fil_ref),
            ("ig", ig_hbm, ig_ref),
            ("val", val_hbm, val_ref),
            ("w", w_hbm, w_ref),
            ("og", og_hbm, og_ref),
            ("across", across_hbm, across_ref),
            ("turn_re", turn_re_hbm, turn_re_ref),
            ("turn_im", turn_im_hbm, turn_im_ref),
            ("within", within_hbm, within_ref),
            ("back", back_hbm, back_ref),
        )
    ):
        loads[name] = pltpu.make_async_copy(src, dst, load_sem.at[i])

    def loaded(*names):
        for name in names:
            loads[name].wait()

    loads["fil"].start()
    loads["cot"].start()

    barrier = pltpu.get_barrier_semaphore()

    def greet(d):
        pl.semaphore_signal(barrier, inc=1, device_id=(lax.rem(me + d, parts), ch), device_id_type=MESH)

    by_fours(1, parts, greet)
    pl.semaphore_signal(barrier, inc=1, device_id=(me, core_peer), device_id_type=MESH)
    pl.semaphore_signal(barrier, inc=1, device_id=(me, y_peer), device_id_type=MESH)

    for name, load in loads.items():
        if name not in ("fil", "cot"):
            load.start()

    def message(p):
        return pl.ds(pl.multiple_of(p * msg, msg), msg)

    near_parts = parts // 2
    side, place = me // near_parts, lax.rem(me, near_parts)

    def send(slot, crossing, back=False, landing=None):
        landing = rcv.at[slot] if landing is None else landing
        base = (1 - side if crossing else side) * near_parts

        def start(i):
            p = base + lax.rem(place + i * 13, near_parts)
            by_channel = lax.rem(p, tiles) * groups + p // tiles
            pltpu.make_async_remote_copy(
                src_ref=snd.at[slot, message(p if back else by_channel)],
                dst_ref=landing.at[message(my_slot if back else me)],
                send_sem=snd_sem.at[slot],
                recv_sem=rcv_sem.at[slot],
                device_id=(p, ch),
                device_id_type=MESH,
            ).start()

        by_fours(0 if crossing else 1, near_parts, start)

    def await_bytes(ref, sem):
        ref = ref.at[pl.ds(0, (parts - 1) * msg)]
        pltpu.make_async_copy(ref, ref, sem).wait()

    def arrived(slot):
        await_bytes(rcv.at[slot], rcv_sem.at[slot])

    def to_messages(slot, first, second, row):
        n = first.shape[0] // GROUP
        both = jnp.concatenate([first.reshape(n, GROUP, half), second.reshape(n, GROUP, half)], 1)
        snd[slot, pl.ds(row, n * msg)] = both.reshape(n * msg, half).astype(BF16)

    def pack(slot, load):
        def go(t, _):
            cols = pl.ds(pl.multiple_of(t * tile, tile), tile)
            first, second = (load(pl.ds(h * half, half), cols).T for h in range(2))
            to_messages(slot, first, second, pl.multiple_of(t * groups * msg, groups * msg))
            return 0

        lax.fori_loop(0, tiles, go, 0)
        rcv[slot, message(me)] = snd[slot, message(my_slot)]

    def turn(real, imag, cols):
        a, b = turn_re_ref[:, cols], turn_im_ref[:, cols]
        return real * a - imag * b, real * b + imag * a

    def put_lhs(real, imag, cols, cols_imag, fine):
        for value, at in ((real, cols), (imag, cols_imag)):
            if fine:
                hi, lo = split_value(value)
                lhs[:nk, at] = hi
                lhs[nk:, at] = lo
            else:
                lhs[:nk, at] = value.astype(BF16)

    def halves_of(h):
        return (
            pl.ds(pl.multiple_of(h * half, half), half),
            pl.ds(pl.multiple_of(rows + h * half, half), half),
        )

    def within(dst, fine):
        def go(j, _):
            cols = pl.ds(pl.multiple_of(j * half, half), half)
            if fine:
                both = jnp.dot(lhs[...], within_ref[:, cols], preferred_element_type=F32)
                spec[dst, :, cols] = both[:nk] + both[nk:]
            else:
                spec[dst, :, cols] = jnp.dot(lhs[:nk], within_ref[:, cols], preferred_element_type=F32)
            return 0

        lax.fori_loop(0, 4, go, 0)

    step = min(16, parts)

    def forward(slot, dst, fine):
        def regroup(i, _):
            both = rcv[slot, pl.ds(pl.multiple_of(i * step * msg, step * msg), step * msg)]
            both = both.astype(F32).reshape(step, msg, half)
            at = pl.ds(pl.multiple_of(i * step * GROUP, step * GROUP), step * GROUP)
            chan_buf[at, :half] = both[:, :GROUP].reshape(step * GROUP, half).astype(BF16)
            chan_buf[at, half:] = both[:, GROUP:].reshape(step * GROUP, half).astype(BF16)
            return 0

        lax.fori_loop(0, parts // step, regroup, 0)

        def go(h, _):
            cols, cols_imag = halves_of(h)
            if fine:
                y = jnp.dot(across_ref[...], chan_buf[:, cols], preferred_element_type=F32)
                y = y[: 2 * nk] + y[2 * nk :]
            else:
                y = jnp.dot(across_ref[: 2 * nk], chan_buf[:, cols], preferred_element_type=F32)
            real, imag = turn(y[:nk], y[nk:], cols)
            put_lhs(real, imag, cols, cols_imag, True)
            return 0

        lax.fori_loop(0, 2, go, 0)
        within(dst, True)

    def inverse(slot, product, fine):
        def fill(h, _):
            cols, cols_imag = halves_of(h)
            real, imag = product(cols, cols_imag)
            put_lhs(real, imag, cols, cols_imag, fine)
            return 0

        lax.fori_loop(0, 2, fill, 0)
        within(3, fine)

        def go(h, _):
            cols, cols_imag = halves_of(h)
            real, imag = turn(spec[3, :, cols], spec[3, :, cols_imag], cols)
            for i, value in enumerate((real, imag)):
                hi, lo = split_value(value)
                stack[i * nk : (i + 1) * nk, cols] = hi
                stack[(2 + i) * nk : (3 + i) * nk, cols] = hi
                if fine:
                    stack[(4 + i) * nk : (5 + i) * nk, cols] = lo
            if fine:
                time_buf[:, cols] = jnp.dot(back_ref[...], stack[:, cols], preferred_element_type=F32)
            else:
                time_buf[:, cols] = jnp.dot(
                    back_ref[:, : 4 * nk], stack[: 4 * nk, cols], preferred_element_type=F32
                )
            return 0

        lax.fori_loop(0, 2, go, 0)

        def regroup(i, _):
            at = pl.ds(pl.multiple_of(i * step * GROUP, step * GROUP), step * GROUP)
            to_messages(slot, time_buf[at, :half], time_buf[at, half:], pl.multiple_of(i * step * msg, step * msg))
            return 0

        lax.fori_loop(0, parts // step, regroup, 0)

    def to_chan(i, src, dst, peer, snd_sems, rcv_sems):
        return pltpu.make_async_remote_copy(
            src_ref=src, dst_ref=dst, send_sem=snd_sems.at[i], recv_sem=rcv_sems.at[i],
            device_id=(me, peer), device_id_type=MESH,
        )

    def cot_copy(i, owner, h, peer):
        ref = cots.at[owner, pl.ds(h * (blk // 2), blk // 2)]
        return to_chan(i, ref, ref, peer, cot_snd_sem, cot_rcv_sem)

    cot_y = [cot_copy(h, ch, h, y_peer) for h in range(2)]
    cot_core = to_chan(2, cots.at[ch], cots.at[ch], core_peer, cot_snd_sem, cot_rcv_sem)
    cot_far = [cot_copy(3 + h, y_peer, h, core_peer) for h in range(2)]

    loaded("fil")
    pack(K_SLOT, lambda r, c: fil_ref[r, c].astype(F32))
    loaded("cot")
    pl.semaphore_wait(barrier, parts + 1)
    cot_y[0].start()
    cot_y[1].start()
    cot_core.start()
    send(K_SLOT, False)
    loaded("ig", "val")

    def source(r, c):
        return ig_ref[r, c].astype(F32) * val_ref[r, c].astype(F32)

    pack(S_SLOT, source)
    send(S_SLOT, False)
    send(K_SLOT, True)
    loaded("w", "og")

    def d_block(b):
        at = pl.ds(pl.multiple_of(b * blk, blk), blk)
        d = lax.dot_general(cots[b], w_ref[...], (((1,), (1,)), ((), ())), preferred_element_type=F32)
        d_gated[at] = d
        time_buf[at] = d * og_ref[at].astype(F32)

    d_block(ch)
    cot_core.wait_recv()
    d_block(core_peer)
    for h in range(2):
        cot_y[h].wait_recv()
        cot_far[h].start()
    send(S_SLOT, True)
    d_block(y_peer)
    cot_far[0].wait_recv()
    cot_far[1].wait_recv()
    d_block(far_peer)
    pack(D_SLOT, lambda r, c: time_buf[r, c])
    send(D_SLOT, False)

    loaded("across", "turn_re", "turn_im", "within", "back")
    arrived(K_SLOT)
    forward(K_SLOT, 0, True)
    send(D_SLOT, True)
    arrived(S_SLOT)
    forward(S_SLOT, 1, True)

    def conv_product(cols, cols_imag):
        a, b = spec[0, :, cols], spec[0, :, cols_imag]
        c, d = spec[1, :, cols], spec[1, :, cols_imag]
        return a * c - b * d, -(a * d + b * c)

    inverse(C_SLOT, conv_product, True)
    send(C_SLOT, False, back=True)
    send(C_SLOT, True, back=True)
    rcv[C_SLOT, message(my_slot)] = snd[C_SLOT, message(me)]
    arrived(D_SLOT)
    forward(D_SLOT, 2, False)

    def correlation(which):
        def product(cols, cols_imag):
            a, b = spec[which, :, cols], spec[which, :, cols_imag]
            c, d = spec[2, :, cols], spec[2, :, cols_imag]
            return a * c + b * d, b * c - a * d

        return product

    inverse(DS_SLOT, correlation(0), False)
    send(DS_SLOT, True, back=True)
    send(DS_SLOT, False, back=True)
    rcv[DS_SLOT, message(my_slot)] = snd[DS_SLOT, message(me)]

    arrived(C_SLOT)

    def unpack_half(slot, h, store):
        at = pl.ds(pl.multiple_of(h * half, half), half)

        def go(t, _):
            cols = pl.ds(pl.multiple_of(t * tile, tile), tile)
            both = rcv[slot, pl.ds(pl.multiple_of(t * groups * msg, groups * msg), groups * msg)]
            both = both.astype(F32).reshape(groups, msg, half)
            store(at, cols, jnp.where(h == 0, both[:, :GROUP], both[:, GROUP:]).reshape(tile, half).T)
            return 0

        lax.fori_loop(0, tiles, go, 0)

    def use_conv(h):
        def store(at, cols, conv):
            gated[at, cols] = (og_ref[at, cols].astype(F32) * conv).astype(BF16)
            d_og_buf[at, cols] = (d_gated[at, cols] * conv).astype(BF16)

        unpack_half(C_SLOT, h, store)

    out_tile = min(512, dout)

    def project(j, of_core, store):
        at = pl.ds(pl.multiple_of((2 * j + of_core) * blk, blk), blk)

        def go(n, _):
            cols = pl.ds(pl.multiple_of(n * out_tile, out_tile), out_tile)
            store(cols, jnp.dot(gated[at], w_ref[:, cols], preferred_element_type=F32))
            return 0

        lax.fori_loop(0, dout // out_tile, go, 0)

    def store_peer(i):
        def store(cols, value):
            core_snd[i, :, cols] = value.astype(BF16)

        return store

    def store_mine(i):
        def store(cols, value):
            total_buf[i, :, cols] = value

        return store

    red_core = [to_chan(i, core_snd.at[i], core_rcv.at[i], core_peer, red_snd_sem, red_rcv_sem) for i in range(2)]
    red_y = to_chan(2, y_snd, y_rcv, y_peer, red_snd_sem, red_rcv_sem)
    use_conv(1 - high)
    project(1 - high, 1 - core, store_peer(0))
    red_core[0].start()
    project(1 - high, core, store_mine(0))
    red_core[0].wait_recv()
    y_snd[...] = (total_buf[0] + core_rcv[0].astype(F32)).astype(BF16)
    red_y.start()
    inverse(DK_SLOT, correlation(1), False)
    own_dk = pltpu.make_async_copy(snd.at[DK_SLOT, message(me)], dk_hbm.at[message(my_slot)], store_sem.at[1])
    own_dk.start()
    send(DK_SLOT, False, back=True, landing=dk_hbm)
    send(DK_SLOT, True, back=True, landing=dk_hbm)
    use_conv(high)
    d_og_out = pltpu.make_async_copy(d_og_buf, d_og_hbm, store_sem.at[2])
    d_og_out.start()
    project(high, 1 - core, store_peer(1))
    red_core[1].start()
    project(high, core, store_mine(1))
    red_core[1].wait_recv()
    total_buf[1] = total_buf[1] + core_rcv[1].astype(F32)
    red_y.wait_recv()
    out_buf[...] = (total_buf[1] + y_rcv[...].astype(F32)).astype(BF16)
    out_out = pltpu.make_async_copy(out_buf, out_hbm, store_sem.at[3])
    out_out.start()

    def use_source(at, cols, grad):
        ds_buf[at, cols] = grad.astype(BF16)

    arrived(DS_SLOT)
    for h in range(2):
        unpack_half(DS_SLOT, h, use_source)
    ds_out = pltpu.make_async_copy(ds_buf, ds_hbm, store_sem.at[0])
    ds_out.start()
    for slot in range(6):
        await_bytes(snd.at[slot], snd_sem.at[slot])
    for copy in (*cot_y, cot_core, *cot_far, *red_core, red_y):
        copy.wait_send()
    for copy in (ds_out, own_dk, d_og_out, out_out):
        copy.wait()
    await_bytes(dk_hbm, rcv_sem.at[DK_SLOT])


def finish(
    ig_hbm, val_hbm, ds_hbm, dk_hbm, d_og_in_hbm, out_in_hbm,
    d_ig_hbm, d_val_hbm, d_fil_hbm, d_og_hbm, out_hbm,
    ig, val, ds, dk, d_og_in, out, d_ig, d_val, d_fil, d_og, load_sem, store_sem,
):
    rows, width = ig.shape
    half = rows // 2
    loads, stores = [], []

    def load(src, dst):
        loads.append(pltpu.make_async_copy(src, dst, load_sem.at[len(loads)]))
        loads[-1].start()

    def store(src, dst):
        stores.append(pltpu.make_async_copy(src, dst, store_sem.at[len(stores)]))
        stores[-1].start()

    halves = [pl.ds(h * half, half) for h in range(2)]
    for at in halves:
        for src, dst in ((ds_hbm, ds), (val_hbm, val), (ig_hbm, ig)):
            load(src.at[at], dst.at[at])
    load(dk_hbm, dk)
    load(d_og_in_hbm, d_og_in)
    load(out_in_hbm, out)
    for h, at in enumerate(halves):
        for copy in loads[3 * h : 3 * h + 3]:
            copy.wait()
        grad = ds[at].astype(F32)
        d_ig[at] = grad * val[at].astype(F32)
        store(d_ig.at[at], d_ig_hbm.at[at])
        d_val[at] = grad * ig[at].astype(F32)
        store(d_val.at[at], d_val_hbm.at[at])
    tile = min(TILE, width)
    msgs = 2 * tile
    loads[6].wait()
    for h, at in enumerate(halves):
        for t in range(width // tile):
            both = dk[pl.ds(t * msgs, msgs)].astype(F32).reshape(tile // GROUP, 2 * GROUP, half)
            d_fil[at, pl.ds(t * tile, tile)] = both[:, h * GROUP : (h + 1) * GROUP].reshape(tile, half).T
        store(d_fil.at[at], d_fil_hbm.at[at])
    loads[8].wait()
    store(out, out_hbm)
    loads[7].wait()
    d_og[...] = d_og_in[...].astype(F32)
    store(d_og, d_og_hbm)
    for copy in stores:
        copy.wait()


def on_device(out_gate, in_gate, values, filter_param, out_weight, out_cotangent):
    rows, width = values.shape
    parts = lax.axis_size("seq")
    blk, dout = out_cotangent.shape
    tables = make_tables(parts, rows)
    nk = tables[3].shape[0]
    msgs = (parts * 2 * GROUP, rows // 2)
    operands = (out_gate, in_gate, values, filter_param, out_weight, out_cotangent, *tables)
    grad = jax.ShapeDtypeStruct((rows, width), F32)
    block_out = jax.ShapeDtypeStruct((blk, dout), BF16)
    raw = jax.ShapeDtypeStruct(msgs, BF16)
    short = jax.ShapeDtypeStruct((rows, width), BF16)
    anywhere = pl.BlockSpec(memory_space=pl.ANY)
    output, d_og, ds_raw, dk_raw = pl.pallas_call(
        kernel,
        out_shape=(block_out, short, short, raw),
        in_specs=[anywhere] * 11,
        out_specs=(anywhere,) * 4,
        scratch_shapes=[
            *(pltpu.VMEM(x.shape, x.dtype) for i, x in enumerate(operands) if i != 5),
            pltpu.VMEM((6, *msgs), BF16),
            pltpu.VMEM((5, *msgs), BF16),
            pltpu.VMEM((4, blk, dout), BF16),
            pltpu.VMEM((rows, width), F32),
            pltpu.VMEM((rows, width), F32),
            pltpu.VMEM((rows, width), BF16),
            pltpu.VMEM((rows, width), BF16),
            pltpu.VMEM((rows, width), BF16),
            pltpu.VMEM((parts * GROUP, rows), BF16),
            pltpu.VMEM((2 * nk, 2 * rows), BF16),
            pltpu.VMEM((4, nk, 2 * rows), F32),
            pltpu.VMEM((6 * nk, rows), BF16),
            pltpu.VMEM((2, blk, dout), BF16),
            pltpu.VMEM((2, blk, dout), BF16),
            pltpu.VMEM((blk, dout), BF16),
            pltpu.VMEM((blk, dout), BF16),
            pltpu.VMEM((2, blk, dout), F32),
            pltpu.VMEM((blk, dout), BF16),
            pltpu.SemaphoreType.DMA((11,)),
            pltpu.SemaphoreType.DMA((4,)),
            pltpu.SemaphoreType.DMA((6,)),
            pltpu.SemaphoreType.DMA((6,)),
            pltpu.SemaphoreType.DMA((5,)),
            pltpu.SemaphoreType.DMA((5,)),
            pltpu.SemaphoreType.DMA((3,)),
            pltpu.SemaphoreType.DMA((3,)),
        ],
        compiler_params=pltpu.CompilerParams(collective_id=0, has_side_effects=True, vmem_limit_bytes=60 * 2**20),
    )(*operands)
    d_ig, d_val, d_fil, d_og, output = pl.pallas_call(
        finish,
        out_shape=(grad, grad, grad, grad, block_out),
        in_specs=[anywhere] * 6,
        out_specs=(anywhere,) * 5,
        scratch_shapes=[
            *([pltpu.VMEM((rows, width), BF16)] * 3),
            pltpu.VMEM(msgs, BF16),
            pltpu.VMEM((rows, width), BF16),
            pltpu.VMEM((blk, dout), BF16),
            *([pltpu.VMEM((rows, width), F32)] * 4),
            pltpu.SemaphoreType.DMA((9,)),
            pltpu.SemaphoreType.DMA((8,)),
        ],
        compiler_params=pltpu.CompilerParams(vmem_limit_bytes=60 * 2**20),
    )(in_gate, values, ds_raw, dk_raw, d_og, output)
    return output, d_og, d_ig, d_val, d_fil


def solution(mesh):
    return jax.shard_map(
        on_device,
        mesh=mesh,
        in_specs=(
            P("seq", "chan"),
            P("seq", "chan"),
            P("seq", "chan"),
            P("seq", "chan"),
            P("chan", None),
            P(("seq", "chan"), None),
        ),
        out_specs=(
            P(("seq", "chan"), None),
            P("seq", "chan"),
            P("seq", "chan"),
            P("seq", "chan"),
            P("seq", "chan"),
        ),
        check_vma=False,
    )
```
